256 devices in a mesh: date: 8 (over z_hi, x), space: 32 (over z_lo, y, core).
Axes of the slice: x: 4, y: 4, z: 8 (z_hi: 2, z_lo: 4; z = z_hi * 4 + z_lo), core: 2. Of those that a mesh axis runs over, the one named last changes fastest.
Arguments:
- stack: bfloat16 [32, 4096, 1280], P('date', 'space'), may hold values from -16 to 16
- w_qkv: bfloat16 [1280, 3840], P('space'), may hold values from -0.15625 to 0.15625
- w_out: bfloat16 [1280, 1280], P('space'), may hold values from -0.15625 to 0.15625
- conv_weight: float32 [3, 3, 1280], replicated, may hold values from -1 to 1
- conv_bias: float32 [1280], replicated, may hold values from -3 to 3
Outputs:
- output: bfloat16 [32, 4096, 1280], P('date', 'space')
The draws below stay inside these ranges and needn't reach their ends.
All inputs are finite; a program needn't handle non-finite values.
Results may differ from the reference program's by a relative error of at most 0.013.
Values may be sent and summed in bfloat16 or wider, within the bound.
No kernel may reach another device: no remote copies, remote signals or barrier semaphores. Data moves between devices by JAX's collectives and lax.ppermute only.
A program may use at most 64 MiB of HBM per device.

```python
import math
import jax
import jax.numpy as jnp
from jax import lax

D = 1280
HEADS = 16
HEAD = 80
DATES = 32
GRID = 64
PATCHES = 4096


def draw_stack(key, part):
    key = jax.random.fold_in(key, 11)
    shape = (DATES, PATCHES, D)
    values = jnp.clip(jax.random.normal(key, shape, jnp.float32), -6.0, 6.0)
    return values.astype(jnp.bfloat16)


def block_scale(stream_key, shape, pieces, least, largest):
    def one(axis_at, blocks):
        draws = jax.random.uniform(jax.random.fold_in(jax.random.fold_in(stream_key, 6), axis_at), (blocks,), jnp.float32, least / len(pieces), largest / len(pieces))
        return jnp.repeat(jnp.exp(draws), shape[axis_at] // blocks).reshape((-1,) + (1,) * (len(shape) - axis_at - 1))

    loudness = one(*pieces[0])
    for cut in pieces[1:]:
        loudness = loudness * one(*cut)
    return loudness


def gaussian(stream_key, shape, scale, bound, cuts=(), dtype=jnp.bfloat16):
    array = jax.random.normal(stream_key, shape, jnp.float32) * scale
    if len(cuts) > 0:
        array = block_scale(stream_key, shape, cuts, -0.22, 0.18) * array
    return jnp.clip(array, min=-bound, max=bound).astype(dtype)


def setup_inputs(seed: int = 0) -> dict:
    key_of = jax.random.split(jax.random.key(seed), 6)
    stack = draw_stack(jax.random.fold_in(key_of[5], 71), 0)
    w_qkv = gaussian(key_of[1], (D, 3 * D), D ** -0.5, 0.15625, ((0, 32),))
    w_out = gaussian(key_of[2], (D, D), D ** -0.5, 0.15625, ((0, 32),))
    conv_weight = gaussian(key_of[3], (3, 3, D), 0.25, 1.0, (), jnp.float32)
    conv_bias = gaussian(key_of[4], (D,), 0.5, 3.0, (), jnp.float32)
    return {"stack": stack, "w_qkv": w_qkv, "w_out": w_out, "conv_weight": conv_weight, "conv_bias": conv_bias}


def reference(stack, w_qkv, w_out, conv_weight, conv_bias):
    flat_rows = stack.reshape(DATES * PATCHES, D)
    head_weights = w_qkv.reshape(D, 3, HEADS, HEAD).transpose(2, 0, 1, 3).reshape(HEADS, D, 3 * HEAD)

    def one_head(weight_head):
        projected = jnp.dot(flat_rows, weight_head, preferred_element_type=jnp.float32).astype(jnp.bfloat16)
        projected = projected.reshape(DATES, PATCHES, 3 * HEAD)
        queries = projected[:, :, :HEAD].astype(jnp.float32)
        keys_all = projected[:, :, HEAD:2 * HEAD].astype(jnp.float32)
        values_all = projected[:, :, 2 * HEAD:].astype(jnp.float32)
        scores = jnp.einsum('tpe,spe->pts', queries, keys_all) / math.sqrt(HEAD)
        weights = jax.nn.softmax(scores, axis=-1).astype(jnp.bfloat16)
        attended = jnp.einsum('pts,spe->tpe', weights.astype(jnp.float32), values_all)
        return attended.astype(jnp.bfloat16)
    heads_out = lax.map(one_head, head_weights)
    attended = heads_out.transpose(1, 2, 0, 3).reshape(DATES, PATCHES, D)

    def project_date(pair):
        attended_date, stack_date = pair
        total = jnp.dot(attended_date, w_out, preferred_element_type=jnp.float32)
        return (total + stack_date.astype(jnp.float32)).astype(jnp.bfloat16)
    mixed = lax.map(project_date, (attended, stack))

    def convolve(mixed_date):
        grid_vals = mixed_date.reshape(GRID, GRID, D).astype(jnp.float32)
        padded = jnp.pad(grid_vals, ((1, 1), (1, 1), (0, 0)))
        total = grid_vals + conv_bias
        for row_off in range(3):
            for col_off in range(3):
                total = total + conv_weight[row_off, col_off] * padded[row_off:row_off + GRID, col_off:col_off + GRID]
        return total.astype(jnp.bfloat16).reshape(PATCHES, D)
    return lax.map(convolve, mixed)
```

```python
import functools
import math

import jax
import jax.numpy as jnp
from jax import lax
from jax.experimental import pallas as pl
from jax.experimental.pallas import tpu as pltpu
from jax.sharding import Mesh
from jax.sharding import PartitionSpec as P

HEADS = 16
GROUP = 8
BF16 = jnp.bfloat16
F32 = jnp.float32


def dot(a, b):
    return jnp.dot(a, b, preferred_element_type=F32)


def attend_rows(queries, keys, values, head_size):
    width = queries.shape[1]
    rows, cols = queries.shape[0], keys.shape[0]
    same = (
        lax.broadcasted_iota(jnp.int32, (rows, cols), 0) % GROUP
        == lax.broadcasted_iota(jnp.int32, (rows, cols), 1) % GROUP
    )
    tiles = [None] * (width // 128)
    for head in range(width // head_size):
        start, stop = head * head_size, (head + 1) * head_size
        first, last = start // 128, -(-stop // 128)
        window = slice(first * 128, last * 128)
        lane = lax.broadcasted_iota(jnp.int32, (rows, (last - first) * 128), 1) + first * 128
        inside = (lane >= start) & (lane < stop)
        query = jnp.where(inside, queries[:, window], jnp.zeros((), BF16))
        scores = lax.dot_general(
            query, keys[:, window], (((1,), (1,)), ((), ())), preferred_element_type=F32
        )
        scores = jnp.where(same, scores * (1.0 / math.sqrt(head_size)), -jnp.inf)
        exps = jnp.exp(scores - jnp.max(scores, axis=1, keepdims=True))
        weights = (exps * (1.0 / jnp.sum(exps, axis=1, keepdims=True))).astype(BF16)
        out = dot(weights, values[:, window])
        out = jnp.where(inside, out, 0.0)
        for tile in range(first, last):
            part = out[:, (tile - first) * 128 : (tile - first + 1) * 128]
            tiles[tile] = part if tiles[tile] is None else tiles[tile] + part
    return jnp.concatenate(tiles, axis=1).astype(BF16)


def block_kernel(head_size, *refs):
    blocks, w_hbm, out, x_vm, w_vm, q_vm, k_vm, v_vm, att, x_sem, w_sem = (
        refs[:8],
        *refs[8:],
    )
    half = w_vm.shape[-1]
    width = 2 * half
    x_copies = [
        pltpu.make_async_copy(block, x_vm.at[i], x_sem.at[i]) for i, block in enumerate(blocks)
    ]
    w_copies = {
        (mat, core, col): pltpu.make_async_copy(
            w_hbm.at[mat, col, core], w_vm.at[mat, core, :, col], w_sem.at[mat, core, col]
        )
        for core in range(2)
        for mat in range(4)
        for col in range(4)
    }
    for copy in x_copies:
        copy.start()
    for copy in w_copies.values():
        copy.start()
    for copy in x_copies:
        copy.wait()

    def wait_w(mat, core):
        for col in range(4):
            w_copies[mat, core, col].wait()

    for core in range(2):
        for mat, into, count in ((0, q_vm, 4), (1, k_vm, 8), (2, v_vm, 8)):
            wait_w(mat, core)

            def project(i, _, mat=mat, into=into):
                x = x_vm[pl.ds(i * 2, 2)].reshape(-1, width)
                w = w_vm[mat, core].reshape(width, half)
                into[pl.ds(i * 2, 2)] = dot(x, w).astype(BF16).reshape(2, 4, -1, half)
                return _

            lax.fori_loop(0, count // 2, project, 0)

        def attend(group, _):
            got = attend_rows(
                q_vm[:, pl.ds(group, 1)].reshape(-1, half),
                k_vm[:, pl.ds(group, 1)].reshape(-1, half),
                v_vm[:, pl.ds(group, 1)].reshape(-1, half),
                head_size,
            )
            att[:, pl.ds(group, 1), :, core * half : (core + 1) * half] = got.reshape(4, 1, -1, half)
            return _

        lax.fori_loop(0, 4, attend, 0)

    for core in range(2):
        wait_w(3, core)

        def mix(i, _):
            a = att[pl.ds(i * 2, 2)].reshape(-1, width)
            w = w_vm[3, core].reshape(width, half)
            cut = slice(core * half, (core + 1) * half)
            x = x_vm[pl.ds(i * 2, 2), :, cut].reshape(-1, half)
            total = dot(a, w) + x.astype(F32)
            out[pl.ds(i * 2, 2), :, cut] = total.astype(BF16).reshape(2, -1, half)
            return _

        lax.fori_loop(0, 2, mix, 0)


def run_block(blocks, w_all, head_size):
    rows, width = blocks[0].shape
    half = width // 2
    hbm = pl.BlockSpec(memory_space=pl.ANY)
    return pl.pallas_call(
        functools.partial(block_kernel, head_size),
        out_shape=jax.ShapeDtypeStruct((4, rows, width), BF16),
        in_specs=[hbm] * 9,
        out_specs=pl.BlockSpec(memory_space=pltpu.VMEM),
        scratch_shapes=[
            pltpu.VMEM((8, rows, width), BF16),
            pltpu.VMEM((4, 2, 4, 4, width // 16, half), BF16),
            pltpu.VMEM((4, 4, rows // 4, half), BF16),
            pltpu.VMEM((8, 4, rows // 4, half), BF16),
            pltpu.VMEM((8, 4, rows // 4, half), BF16),
            pltpu.VMEM((4, 4, rows // 4, width), BF16),
            pltpu.SemaphoreType.DMA((8,)),
            pltpu.SemaphoreType.DMA((4, 2, 4)),
        ],
        compiler_params=pltpu.CompilerParams(vmem_limit_bytes=48 * 1024 * 1024),
    )(*blocks, w_all)


def ring(count, shift):
    return [(i, (i + shift) % count) for i in range(count)]


def gather_weights(w_qkv, w_out):
    rows, width = w_out.shape
    half = width // 2
    x, zl, core = lax.axis_index("x"), lax.axis_index("zl"), lax.axis_index("c")
    joined = jnp.concatenate(
        [w_qkv.reshape(rows, 3, 2, half), w_out.reshape(rows, 1, 2, half)], axis=1
    )
    mine = lax.dynamic_index_in_dim(joined, x, 1, keepdims=False)
    keep = lax.dynamic_index_in_dim(mine, core, 1, keepdims=False)
    give = lax.dynamic_index_in_dim(mine, 1 - core, 1, keepdims=False)
    other = lax.ppermute(give, "c", ring(2, 1))
    piece = jnp.zeros((2, rows, half), BF16)
    piece = lax.dynamic_update_index_in_dim(piece, keep, core, 0)
    piece = lax.dynamic_update_index_in_dim(piece, other, 1 - core, 0).reshape(2 * rows, half)
    planes = jnp.zeros((4, 2 * rows, half), BF16)
    planes = lax.dynamic_update_index_in_dim(planes, piece, zl, 0)
    for shift in (1, 7, 2):
        got = lax.ppermute(piece, ("zh", "zl"), ring(8, shift))
        planes = lax.dynamic_update_index_in_dim(planes, got, (zl + 8 - shift) % 4, 0)
    gathered = lax.all_gather(planes, ("x", "y", "c"), axis=0, tiled=False)
    return gathered.reshape(4, 4, 2, 4, 2 * rows, half)


def shards(stack, w_qkv, w_out, conv_weight, conv_bias):
    date_dev, patch_dev, width = stack.shape
    head_size = width // HEADS
    x = lax.axis_index("x")
    part = patch_dev // 4

    def cut(shift):
        block = lax.dynamic_slice_in_dim(stack, ((x + shift) % 4) * part, part, axis=1)
        block = block.reshape(date_dev, part // GROUP, GROUP, width).transpose(1, 0, 2, 3)
        return block.reshape(date_dev * part, width)

    shifts = (0, 1, 3, 2)
    own = [cut(0)] + [lax.ppermute(cut(s), "x", ring(4, s)) for s in shifts[1:]]
    partner = [lax.ppermute(block, ("zh", "zl"), ring(8, 4)) for block in own]
    w_all = gather_weights(w_qkv, w_out)
    mixed_slots = run_block(own + partner, w_all, head_size)

    home = jnp.zeros((4, date_dev * part, width), BF16)
    for slot, s in enumerate(shifts):
        back = mixed_slots[slot]
        if s:
            back = lax.ppermute(back, "x", ring(4, 4 - s))
        home = lax.dynamic_update_index_in_dim(home, back, (x + s) % 4, 0)
    mixed = home.reshape(4, part // GROUP, date_dev, GROUP, width).transpose(2, 0, 1, 3, 4)

    band_rows = 2
    grid_cols = patch_dev // band_rows
    band = mixed.reshape(date_dev, band_rows, grid_cols, width)
    bands = 32
    axes = ("zl", "y", "c")
    above = lax.ppermute(band[:, -1:], axes, [(i, i + 1) for i in range(bands - 1)])
    below = lax.ppermute(band[:, :1], axes, [(i + 1, i) for i in range(bands - 1)])
    widened = jnp.concatenate([above, band, below], axis=1)
    padded = jnp.pad(widened.astype(F32), ((0, 0), (0, 0), (1, 1), (0, 0)))
    result = band.astype(F32) + conv_bias
    for row_off in range(3):
        for col_off in range(3):
            result = (
                result
                + conv_weight[row_off, col_off]
                * padded[:, row_off : row_off + band_rows, col_off : col_off + grid_cols]
            )
    return result.astype(BF16).reshape(date_dev, patch_dev, width)


def solution(mesh):
    fine = Mesh(mesh.devices.reshape(2, 4, 4, 4, 2), ("zh", "x", "zl", "y", "c"))
    date, space = ("zh", "x"), ("zl", "y", "c")
    in_specs = (P(date, space, None), P(space, None), P(space, None), P(), P())
    out_specs = P(date, space, None)
    return jax.shard_map(
        shards, mesh=fine, in_specs=in_specs, out_specs=out_specs, check_vma=False
    )
```

```python
import functools
import math

import jax
import jax.numpy as jnp
from jax import lax
from jax.experimental import pallas as pl
from jax.experimental.pallas import tpu as pltpu
from jax.sharding import Mesh
from jax.sharding import PartitionSpec as P

HEADS = 16
GROUP = 8
BF16 = jnp.bfloat16
F32 = jnp.float32
Z_SHIFTS = (0, 1, 3, 2)


def dot(a, b):
    return jnp.dot(a, b, preferred_element_type=F32)


def attend_rows(queries, keys, values, head_size):
    width = queries.shape[1]
    rows, cols = queries.shape[0], keys.shape[0]
    same = (
        lax.broadcasted_iota(jnp.int32, (rows, cols), 0) % GROUP
        == lax.broadcasted_iota(jnp.int32, (rows, cols), 1) % GROUP
    )
    tiles = [None] * (width // 128)
    for head in range(width // head_size):
        start, stop = head * head_size, (head + 1) * head_size
        first, last = start // 128, -(-stop // 128)
        window = slice(first * 128, last * 128)
        lane = lax.broadcasted_iota(jnp.int32, (rows, (last - first) * 128), 1) + first * 128
        inside = (lane >= start) & (lane < stop)
        query = jnp.where(inside, queries[:, window], jnp.zeros((), BF16))
        scores = lax.dot_general(
            query, keys[:, window], (((1,), (1,)), ((), ())), preferred_element_type=F32
        )
        scores = jnp.where(same, scores * (1.0 / math.sqrt(head_size)), -jnp.inf)
        exps = jnp.exp(scores - jnp.max(scores, axis=1, keepdims=True))
        weights = (exps * (1.0 / jnp.sum(exps, axis=1, keepdims=True))).astype(BF16)
        out = dot(weights, values[:, window])
        out = jnp.where(inside, out, 0.0)
        for tile in range(first, last):
            part = out[:, (tile - first) * 128 : (tile - first + 1) * 128]
            tiles[tile] = part if tiles[tile] is None else tiles[tile] + part
    return jnp.concatenate(tiles, axis=1).astype(BF16)


def block_kernel(head_size, place, *refs):
    blocks, (own_a, other_a, own_b, other_b) = refs[:8], refs[8:12]
    out, x_vm, w_vm, q_vm, k_vm, v_vm, att, x_sem, w_sem = refs[12:]
    half = w_vm.shape[-1]
    width = 2 * half
    core, zl = place[0], place[1]
    x_copies = [
        pltpu.make_async_copy(block, x_vm.at[i], x_sem.at[i]) for i, block in enumerate(blocks)
    ]
    w_copies = {}
    for side, (part_a, part_b) in enumerate(((own_a, own_b), (other_a, other_b))):
        for mat in range(4):
            for slot, shift in enumerate(Z_SHIFTS):
                part = part_a.at[mat, :, slot] if slot < 2 else part_b.at[:, mat, slot - 2]
                w_copies[side, mat, slot] = pltpu.make_async_copy(
                    part, w_vm.at[side, mat, (zl + 4 - shift) % 4], w_sem.at[side, mat, slot]
                )
    for copy in x_copies:
        copy.start()
    for copy in w_copies.values():
        copy.start()
    for copy in x_copies:
        copy.wait()

    def wait_w(side, mat):
        for slot in range(4):
            w_copies[side, mat, slot].wait()

    for side in range(2):
        at = core if side == 0 else 1 - core
        for mat, into, count in ((0, q_vm, 4), (1, k_vm, 8), (2, v_vm, 8)):
            wait_w(side, mat)

            def project(i, _, mat=mat, into=into):
                x = x_vm[pl.ds(i * 2, 2)].reshape(-1, width)
                w = w_vm[side, mat].reshape(width, half)
                into[pl.ds(i * 2, 2)] = dot(x, w).astype(BF16).reshape(2, 4, -1, half)
                return _

            lax.fori_loop(0, count // 2, project, 0)

        def attend(group, _):
            got = attend_rows(
                q_vm[:, pl.ds(group, 1)].reshape(-1, half),
                k_vm[:, pl.ds(group, 1)].reshape(-1, half),
                v_vm[:, pl.ds(group, 1)].reshape(-1, half),
                head_size,
            )
            att[pl.ds(at, 1), :, pl.ds(group, 1)] = got.reshape(1, 4, 1, -1, half)
            return _

        lax.fori_loop(0, 4, attend, 0)

    for side in range(2):
        wait_w(side, 3)
        at = core if side == 0 else 1 - core

        def mix(i, _):
            w = w_vm[side, 3].reshape(2, half, half)
            total = dot(att[0, pl.ds(i * 2, 2)].reshape(-1, half), w[0])
            total += dot(att[1, pl.ds(i * 2, 2)].reshape(-1, half), w[1])
            cut = pl.ds(pl.multiple_of(at * half, 128), half)
            total += x_vm[pl.ds(i * 2, 2), :, cut].reshape(-1, half).astype(F32)
            out[pl.ds(i * 2, 2), :, cut] = total.astype(BF16).reshape(2, -1, half)
            return _

        lax.fori_loop(0, 2, mix, 0)


def run_block(place, blocks, weights, head_size):
    rows, width = blocks[0].shape
    half = width // 2
    hbm = pl.BlockSpec(memory_space=pl.ANY)
    return pl.pallas_call(
        functools.partial(block_kernel, head_size),
        out_shape=jax.ShapeDtypeStruct((4, rows, width), BF16),
        in_specs=[pl.BlockSpec(memory_space=pltpu.SMEM)] + [hbm] * 12,
        out_specs=pl.BlockSpec(memory_space=pltpu.VMEM),
        scratch_shapes=[
            pltpu.VMEM((8, rows, width), BF16),
            pltpu.VMEM((2, 4, 4, 4, width // 16, half), BF16),
            pltpu.VMEM((4, 4, rows // 4, half), BF16),
            pltpu.VMEM((8, 4, rows // 4, half), BF16),
            pltpu.VMEM((8, 4, rows // 4, half), BF16),
            pltpu.VMEM((2, 4, 4, rows // 4, half), BF16),
            pltpu.SemaphoreType.DMA((8,)),
            pltpu.SemaphoreType.DMA((2, 4, 4)),
        ],
        compiler_params=pltpu.CompilerParams(vmem_limit_bytes=48 * 1024 * 1024),
    )(place, *blocks, *weights)


def ring(count, shift):
    return [(i, (i + shift) % count) for i in range(count)]


def put(into, piece, at):
    return lax.dynamic_update_index_in_dim(into, piece, at, 0)


def spread(piece, axis):
    me = lax.axis_index(axis)
    whole = put(jnp.zeros((4, *piece.shape), piece.dtype), piece, me)
    for shift in (1, 3, 2):
        whole = put(whole, lax.ppermute(piece, axis, ring(4, shift)), (me + 4 - shift) % 4)
    return whole


def spread_ring(piece, axis):
    me = lax.axis_index(axis)
    half = piece.shape[0] // 2
    left = lax.ppermute(piece, axis, ring(4, 1))
    right = lax.ppermute(piece, axis, ring(4, 3))
    far_low = lax.ppermute(left[:half], axis, ring(4, 1))
    far_high = lax.ppermute(right[half:], axis, ring(4, 3))
    whole = put(jnp.zeros((4, *piece.shape), piece.dtype), piece, me)
    whole = put(whole, left, (me + 3) % 4)
    whole = put(whole, right, (me + 1) % 4)
    zeros = (0,) * (piece.ndim - 1)
    whole = lax.dynamic_update_slice(whole, far_low[None], ((me + 2) % 4, 0) + zeros)
    return lax.dynamic_update_slice(whole, far_high[None], ((me + 2) % 4, half) + zeros)


def gather_weights(w_qkv, w_out):
    rows, width = w_out.shape
    half = width // 2
    x, core = lax.axis_index("x"), lax.axis_index("c")
    joined = jnp.concatenate(
        [w_qkv.reshape(rows, 3, 2, half), w_out.reshape(rows, 1, 2, half)], axis=1
    )
    mine = lax.dynamic_index_in_dim(joined, x, 1, keepdims=False)
    keep = lax.dynamic_index_in_dim(mine, core, 1, keepdims=False)
    give = lax.dynamic_index_in_dim(mine, 1 - core, 1, keepdims=False)
    other = lax.ppermute(give, "c", ring(2, 1))
    piece = put(put(jnp.zeros((2, rows, half), BF16), keep, core), other, 1 - core)
    piece = piece.reshape(2 * rows, half)
    planes = [piece] + [lax.ppermute(piece, ("zh", "zl"), ring(8, s if s < 3 else 7)) for s in Z_SHIFTS[1:]]
    part_a = spread_ring(spread(jnp.stack(planes[:2]), "y"), "x")
    part_b = spread_ring(spread(jnp.stack(planes[2:]), "x"), "y")
    return part_a, lax.ppermute(part_a, "c", ring(2, 1)), part_b, lax.ppermute(part_b, "c", ring(2, 1))


def shards(stack, w_qkv, w_out, conv_weight, conv_bias):
    date_dev, patch_dev, width = stack.shape
    head_size = width // HEADS
    x = lax.axis_index("x")
    part = patch_dev // 4

    def cut(shift):
        block = lax.dynamic_slice_in_dim(stack, ((x + shift) % 4) * part, part, axis=1)
        block = block.reshape(date_dev, part // GROUP, GROUP, width).transpose(1, 0, 2, 3)
        return block.reshape(date_dev * part, width)

    shifts = (0, 1, 3, 2)
    own = [cut(0)] + [lax.ppermute(cut(s), "x", ring(4, s)) for s in shifts[1:]]
    partner = [lax.ppermute(block, ("zh", "zl"), ring(8, 4)) for block in own]
    own_a, other_a, own_b, other_b = gather_weights(w_qkv, w_out)
    place = jnp.stack([lax.axis_index("c"), lax.axis_index("zl")]).astype(jnp.int32)
    weights = (own_a, other_a, own_b, other_b)
    mixed_slots = run_block(place, own + partner, weights, head_size)

    home = jnp.zeros((4, date_dev * part, width), BF16)
    for slot, s in enumerate(shifts):
        back = mixed_slots[slot]
        if s:
            back = lax.ppermute(back, "x", ring(4, 4 - s))
        home = lax.dynamic_update_index_in_dim(home, back, (x + s) % 4, 0)
    mixed = home.reshape(4, part // GROUP, date_dev, GROUP, width).transpose(2, 0, 1, 3, 4)

    band_rows = 2
    grid_cols = patch_dev // band_rows
    band = mixed.reshape(date_dev, band_rows, grid_cols, width)
    bands = 32
    axes = ("zl", "y", "c")
    above = lax.ppermute(band[:, -1:], axes, [(i, i + 1) for i in range(bands - 1)])
    below = lax.ppermute(band[:, :1], axes, [(i + 1, i) for i in range(bands - 1)])
    widened = jnp.concatenate([above, band, below], axis=1)
    padded = jnp.pad(widened.astype(F32), ((0, 0), (0, 0), (1, 1), (0, 0)))
    result = band.astype(F32) + conv_bias
    for row_off in range(3):
        for col_off in range(3):
            result = (
                result
                + conv_weight[row_off, col_off]
                * padded[:, row_off : row_off + band_rows, col_off : col_off + grid_cols]
            )
    return result.astype(BF16).reshape(date_dev, patch_dev, width)


def solution(mesh):
    fine = Mesh(mesh.devices.reshape(2, 4, 4, 4, 2), ("zh", "x", "zl", "y", "c"))
    date, space = ("zh", "x"), ("zl", "y", "c")
    in_specs = (P(date, space, None), P(space, None), P(space, None), P(), P())
    out_specs = P(date, space, None)
    return jax.shard_map(
        shards, mesh=fine, in_specs=in_specs, out_specs=out_specs, check_vma=False
    )
```

```python
import functools
import math

import jax
import jax.numpy as jnp
from jax import lax
from jax.experimental import pallas as pl
from jax.experimental.pallas import tpu as pltpu
from jax.sharding import Mesh
from jax.sharding import PartitionSpec as P

HEADS = 16
GROUP = 8
BF16 = jnp.bfloat16
F32 = jnp.float32


def dot(a, b):
    return jnp.dot(a, b, preferred_element_type=F32)


def attend_rows(queries, keys, values, head_size):
    width = queries.shape[1]
    rows, cols = queries.shape[0], keys.shape[0]
    scale = math.log2(math.e) / math.sqrt(head_size)
    same = (
        lax.broadcasted_iota(jnp.int32, (GROUP, cols), 0)
        == lax.broadcasted_iota(jnp.int32, (GROUP, cols), 1) % GROUP
    )
    others = jnp.where(same, 0.0, -jnp.inf)[None]
    ones = jnp.ones((cols, 128), BF16)
    tiles = [None] * (width // 128)
    head, heads = 0, width // head_size
    while head < heads:
        base = head * head_size // 128 * 128
        count = max(1, min((base + 256) // head_size, heads) - head)
        if base + 256 > width:
            base = width - 256
        lane = lax.broadcasted_iota(jnp.int32, (rows, 256), 1) + base
        query = queries[:, base : base + 256]
        stacked = jnp.concatenate(
            [
                jnp.where(
                    (lane >= h * head_size) & (lane < (h + 1) * head_size),
                    query,
                    jnp.zeros((), BF16),
                )
                for h in range(head, head + count)
            ]
        )
        scores = lax.dot_general(
            stacked,
            keys[:, base : base + 256],
            (((1,), (1,)), ((), ())),
            preferred_element_type=F32,
        )
        scores = (scores.reshape(-1, GROUP, cols) + others).reshape(-1, cols)
        top = jnp.max(scores, axis=1, keepdims=True)
        weights = jnp.exp2((scores - top) * scale).astype(BF16)
        total = 1.0 / dot(weights, ones)
        out = dot(weights, values[:, base : base + 256])
        for i, h in enumerate(range(head, head + count)):
            part = slice(i * rows, (i + 1) * rows)
            for tile in range(h * head_size // 128, -(-(h + 1) * head_size // 128)):
                at = tile * 128 - base
                got = out[part, at : at + 128] * total[part]
                if tiles[tile] is None:
                    tiles[tile] = got
                else:
                    lanes = lax.broadcasted_iota(jnp.int32, (rows, 128), 1) + tile * 128
                    tiles[tile] = jnp.where(lanes < h * head_size, tiles[tile], got)
        head += count
    return jnp.concatenate(tiles, axis=1).astype(BF16)


def block_kernel(head_size, first, *refs):
    blocks, w_hbm, out, x_vm, wp_vm, wo_vm, q_vm, k_vm, v_vm, att, x_sem, w_sem = (
        refs[:8],
        *refs[8:],
    )
    width = x_vm.shape[-1]
    half = width // 2
    rows = out.shape[1]
    groups = q_vm.shape[1]
    x_copies = [
        pltpu.make_async_copy(
            block.at[first * rows : (first + 1) * rows],
            x_vm.at[i * rows : (i + 1) * rows],
            x_sem.at[i],
        )
        for i, block in enumerate(blocks)
    ]
    w_copies = {}
    for core in range(2):
        for mat in range(4):
            lanes = slice(mat * half, (mat + 1) * half) if mat < 3 else slice(core * half, (core + 1) * half)
            for col in range(4):
                target = (wp_vm.at[core] if mat < 3 else wo_vm).at[:, col, :, lanes]
                w_copies[mat, core, col] = pltpu.make_async_copy(
                    w_hbm.at[mat, col, core], target, w_sem.at[mat, core, col]
                )
    for copy in x_copies:
        copy.start()
    for copy in w_copies.values():
        copy.start()
    for copy in x_copies:
        copy.wait()

    def wait_w(mat, core):
        for col in range(4):
            w_copies[mat, core, col].wait()

    for core in range(2):
        for mat in range(3):
            wait_w(mat, core)
        w = wp_vm[core].reshape(width, 3 * half)
        got = dot(x_vm[: 4 * rows], w).astype(BF16)
        q_vm[...] = got[:, :half].reshape(q_vm.shape)
        k_vm[:4] = got[:, half:width].reshape(q_vm.shape)
        v_vm[:4] = got[:, width:].reshape(q_vm.shape)
        got = dot(x_vm[4 * rows :], w[:, half:]).astype(BF16)
        k_vm[4:] = got[:, :half].reshape(q_vm.shape)
        v_vm[4:] = got[:, half:].reshape(q_vm.shape)

        def attend(group, _):
            got = attend_rows(
                q_vm[:, pl.ds(group, 1)].reshape(-1, half),
                k_vm[:, pl.ds(group, 1)].reshape(-1, half),
                v_vm[:, pl.ds(group, 1)].reshape(-1, half),
                head_size,
            )
            att[:, pl.ds(group, 1), :, core * half : (core + 1) * half] = got.reshape(4, 1, -1, half)
            return _

        lax.fori_loop(0, groups, attend, 0)

    wait_w(3, 0)
    wait_w(3, 1)
    total = dot(att[...].reshape(-1, width), wo_vm[...].reshape(width, width))
    total += x_vm[: 4 * rows].astype(F32)
    out[...] = total.astype(BF16).reshape(4, rows, width)


def run_block(blocks, w_all, head_size, first, parts):
    rows, width = blocks[0].shape
    half, rows, groups = width // 2, rows // parts, 4 // parts
    hbm = pl.BlockSpec(memory_space=pl.ANY)
    return pl.pallas_call(
        functools.partial(block_kernel, head_size, first),
        out_shape=jax.ShapeDtypeStruct((4, rows, width), BF16),
        in_specs=[hbm] * 9,
        out_specs=pl.BlockSpec(memory_space=pltpu.VMEM),
        scratch_shapes=[
            pltpu.VMEM((8 * rows, width), BF16),
            pltpu.VMEM((2, 4, 4, width // 16, 3 * half), BF16),
            pltpu.VMEM((4, 4, width // 16, width), BF16),
            pltpu.VMEM((4, groups, rows // groups, half), BF16),
            pltpu.VMEM((8, groups, rows // groups, half), BF16),
            pltpu.VMEM((8, groups, rows // groups, half), BF16),
            pltpu.VMEM((4, groups, rows // groups, width), BF16),
            pltpu.SemaphoreType.DMA((8,)),
            pltpu.SemaphoreType.DMA((4, 2, 4)),
        ],
        compiler_params=pltpu.CompilerParams(vmem_limit_bytes=48 * 1024 * 1024),
    )(*blocks, w_all)


def ring(count, shift):
    return [(i, (i + shift) % count) for i in range(count)]


def gather_weights(w_qkv, w_out):
    rows, width = w_out.shape
    half = width // 2
    x, zl, core = lax.axis_index("x"), lax.axis_index("zl"), lax.axis_index("c")
    joined = jnp.concatenate([w_qkv, w_out], axis=1)
    keep = lax.dynamic_slice_in_dim(joined, x * width + core * half, half, 1)
    give = lax.dynamic_slice_in_dim(joined, x * width + (1 - core) * half, half, 1)
    other = lax.ppermute(give, "c", ring(2, 1))
    piece = jnp.where(
        core == 0, jnp.concatenate([keep, other]), jnp.concatenate([other, keep])
    )
    planes = jnp.zeros((4, 2 * rows, half), BF16)
    planes = lax.dynamic_update_index_in_dim(planes, piece, zl, 0)
    for shift in (1, 7, 2):
        got = lax.ppermute(piece, ("zh", "zl"), ring(8, shift))
        planes = lax.dynamic_update_index_in_dim(planes, got, (zl + 8 - shift) % 4, 0)
    gathered = lax.all_gather(planes, ("x", "y", "c"), axis=0, tiled=False)
    return gathered.reshape(4, 4, 2, 4, 2 * rows, half)


def shards(stack, w_qkv, w_out, conv_weight, conv_bias):
    date_dev, patch_dev, width = stack.shape
    head_size = width // HEADS
    x = lax.axis_index("x")
    part = patch_dev // 4

    def cut(shift):
        block = lax.dynamic_slice_in_dim(stack, ((x + shift) % 4) * part, part, axis=1)
        block = block.reshape(date_dev, part // GROUP, GROUP, width).transpose(1, 0, 2, 3)
        return block.reshape(date_dev * part, width)

    shifts = (0, 1, 3, 2)
    own = [cut(0)] + [lax.ppermute(cut(s), "x", ring(4, s)) for s in shifts[1:]]
    partner = [lax.ppermute(block, ("zh", "zl"), ring(8, 4)) for block in own]
    w_all = gather_weights(w_qkv, w_out)
    mixed_slots = run_block(own + partner, w_all, head_size, 0, 1)

    home = jnp.zeros((4, date_dev * part, width), BF16)
    for slot, s in enumerate(shifts):
        back = mixed_slots[slot]
        if s:
            back = lax.ppermute(back, "x", ring(4, 4 - s))
        home = lax.dynamic_update_index_in_dim(home, back, (x + s) % 4, 0)
    mixed = home.reshape(4, part // GROUP, date_dev, GROUP, width).transpose(2, 0, 1, 3, 4)

    band_rows = 2
    grid_cols = patch_dev // band_rows
    band = mixed.reshape(date_dev, band_rows, grid_cols, width)
    bands = 32
    axes = ("zl", "y", "c")
    above = lax.ppermute(band[:, -1:], axes, [(i, i + 1) for i in range(bands - 1)])
    below = lax.ppermute(band[:, :1], axes, [(i + 1, i) for i in range(bands - 1)])
    widened = jnp.concatenate([above, band, below], axis=1)
    padded = jnp.pad(widened.astype(F32), ((0, 0), (0, 0), (1, 1), (0, 0)))
    result = band.astype(F32) + conv_bias
    for row_off in range(3):
        for col_off in range(3):
            result = (
                result
                + conv_weight[row_off, col_off]
                * padded[:, row_off : row_off + band_rows, col_off : col_off + grid_cols]
            )
    return result.astype(BF16).reshape(date_dev, patch_dev, width)


def solution(mesh):
    fine = Mesh(mesh.devices.reshape(2, 4, 4, 4, 2), ("zh", "x", "zl", "y", "c"))
    date, space = ("zh", "x"), ("zl", "y", "c")
    in_specs = (P(date, space, None), P(space, None), P(space, None), P(), P())
    out_specs = P(date, space, None)
    return jax.shard_map(
        shards, mesh=fine, in_specs=in_specs, out_specs=out_specs, check_vma=False
    )
```

```python
import functools
import math

import jax
import jax.numpy as jnp
from jax import lax
from jax.experimental import pallas as pl
from jax.experimental.pallas import tpu as pltpu
from jax.sharding import Mesh
from jax.sharding import PartitionSpec as P

HEADS = 16
GROUP = 8
BF16 = jnp.bfloat16
F32 = jnp.float32


def dot(a, b):
    return jnp.dot(a, b, preferred_element_type=F32)


def attend_rows(queries, keys, values, head_size):
    width = queries.shape[1]
    rows, cols = queries.shape[0], keys.shape[0]
    scale = math.log2(math.e) / math.sqrt(head_size)
    same = (
        lax.broadcasted_iota(jnp.int32, (GROUP, cols), 0)
        == lax.broadcasted_iota(jnp.int32, (GROUP, cols), 1) % GROUP
    )
    others = jnp.where(same, 0.0, -jnp.inf)[None]
    ones = jnp.ones((cols, 128), BF16)
    tiles = [None] * (width // 128)
    head, heads = 0, width // head_size
    while head < heads:
        base = head * head_size // 128 * 128
        count = max(1, min((base + 256) // head_size, heads) - head)
        if base + 256 > width:
            base = width - 256
        lane = lax.broadcasted_iota(jnp.int32, (rows, 256), 1) + base
        query = queries[:, base : base + 256]
        stacked = jnp.concatenate(
            [
                jnp.where(
                    (lane >= h * head_size) & (lane < (h + 1) * head_size),
                    query,
                    jnp.zeros((), BF16),
                )
                for h in range(head, head + count)
            ]
        )
        scores = lax.dot_general(
            stacked,
            keys[:, base : base + 256],
            (((1,), (1,)), ((), ())),
            preferred_element_type=F32,
        )
        scores = (scores.reshape(-1, GROUP, cols) + others).reshape(-1, cols)
        top = jnp.max(scores, axis=1, keepdims=True)
        weights = jnp.exp2((scores - top) * scale).astype(BF16)
        total = 1.0 / dot(weights, ones)
        out = dot(weights, values[:, base : base + 256])
        for i, h in enumerate(range(head, head + count)):
            part = slice(i * rows, (i + 1) * rows)
            for tile in range(h * head_size // 128, -(-(h + 1) * head_size // 128)):
                at = tile * 128 - base
                got = out[part, at : at + 128] * total[part]
                if tiles[tile] is None:
                    tiles[tile] = got
                else:
                    lanes = lax.broadcasted_iota(jnp.int32, (rows, 128), 1) + tile * 128
                    tiles[tile] = jnp.where(lanes < h * head_size, tiles[tile], got)
        head += count
    return jnp.concatenate(tiles, axis=1).astype(BF16)


def weight_copies(w_hbm, core, target, sem):
    half = w_hbm.shape[-1]
    return [
        pltpu.make_async_copy(
            w_hbm.at[mat, row, core],
            target.at[:, row, :, mat * half : (mat + 1) * half],
            sem.at[mat, row],
        )
        for mat in range(3)
        for row in range(4)
    ]


def attend_half(head_size, x_ref, w_ref, out, q_vm, k_vm, v_vm):
    width = x_ref.shape[1]
    half = width // 2
    own = x_ref.shape[0] // 2
    w = w_ref[...].reshape(width, 3 * half)
    got = dot(x_ref[:own], w).astype(BF16)
    q_vm[...] = got[:, :half].reshape(q_vm.shape)
    k_vm[:4] = got[:, half:width].reshape(q_vm.shape)
    v_vm[:4] = got[:, width:].reshape(q_vm.shape)
    got = dot(x_ref[own:], w[:, half:]).astype(BF16)
    k_vm[4:] = got[:, :half].reshape(q_vm.shape)
    v_vm[4:] = got[:, half:].reshape(q_vm.shape)

    def attend(group, _):
        got = attend_rows(
            q_vm[:, pl.ds(group, 1)].reshape(-1, half),
            k_vm[:, pl.ds(group, 1)].reshape(-1, half),
            v_vm[:, pl.ds(group, 1)].reshape(-1, half),
            head_size,
        )
        out[:, pl.ds(group, 1)] = got.reshape(4, 1, -1, half)
        return _

    lax.fori_loop(0, 4, attend, 0)


def first_kernel(head_size, x_ref, w_hbm, out, w_next, w_home, w_vm, q_vm, k_vm, v_vm, *sems):
    sem, next_sem, home_sem = sems
    half = w_hbm.shape[-1]
    now = weight_copies(w_hbm, 0, w_vm, sem)
    later = weight_copies(w_hbm, 1, w_next, next_sem)
    for core in range(2):
        for row in range(4):
            later.append(
                pltpu.make_async_copy(
                    w_hbm.at[3, row, core],
                    w_home.at[:, row, :, core * half : (core + 1) * half],
                    home_sem.at[core, row],
                )
            )
    for copy in now + later:
        copy.start()
    for copy in now:
        copy.wait()
    attend_half(head_size, x_ref, w_vm, out, q_vm, k_vm, v_vm)
    for copy in later:
        copy.wait()


def second_kernel(head_size, x_ref, w_ref, out, q_vm, k_vm, v_vm):
    attend_half(head_size, x_ref, w_ref, out, q_vm, k_vm, v_vm)


def run_halves(x, w_all, head_size):
    rows, width = x.shape
    half, part = width // 2, rows // 32
    vmem = pl.BlockSpec(memory_space=pltpu.VMEM)
    attended = jax.ShapeDtypeStruct((4, 4, part, half), BF16)
    columns = (4, 4, width // 16, 3 * half)
    scratch = [
        pltpu.VMEM((4, 4, part, half), BF16),
        pltpu.VMEM((8, 4, part, half), BF16),
        pltpu.VMEM((8, 4, part, half), BF16),
    ]
    params = pltpu.CompilerParams(vmem_limit_bytes=36 * 1024 * 1024)
    cost = pl.CostEstimate(
        flops=5 * rows * width * half, bytes_accessed=8 * width * half, transcendentals=0
    )
    first, w_next, w_home = pl.pallas_call(
        functools.partial(first_kernel, head_size),
        out_shape=(
            attended,
            pltpu.VMEM(columns, BF16),
            jax.ShapeDtypeStruct((4, 4, width // 16, width), BF16),
        ),
        in_specs=[vmem, pl.BlockSpec(memory_space=pltpu.HBM)],
        out_specs=(vmem, vmem, vmem),
        scratch_shapes=[
            pltpu.VMEM(columns, BF16),
            *scratch,
            pltpu.SemaphoreType.DMA((3, 4)),
            pltpu.SemaphoreType.DMA((3, 4)),
            pltpu.SemaphoreType.DMA((2, 4)),
        ],
        compiler_params=params,
        cost_estimate=cost,
    )(x, w_all)
    second = pl.pallas_call(
        functools.partial(second_kernel, head_size),
        out_shape=attended,
        in_specs=[vmem, vmem],
        out_specs=vmem,
        scratch_shapes=scratch,
        compiler_params=params,
        cost_estimate=pl.CostEstimate(flops=1 << 20, bytes_accessed=1 << 12, transcendentals=0),
    )(x, w_next)
    return [first, second], w_home.reshape(width, width)


def ring(count, shift):
    return [(i, (i + shift) % count) for i in range(count)]


def tied(*values):
    return lax.optimization_barrier(values)


def gather_weights(w_qkv, w_out):
    rows, width = w_out.shape
    half = width // 2
    x, zl, core = lax.axis_index("x"), lax.axis_index("zl"), lax.axis_index("c")
    joined = jnp.concatenate([w_qkv, w_out], axis=1)
    keep = lax.dynamic_slice_in_dim(joined, x * width + core * half, half, 1)
    give = lax.dynamic_slice_in_dim(joined, x * width + (1 - core) * half, half, 1)
    other = lax.ppermute(give, "c", ring(2, 1))
    piece = jnp.where(
        core == 0, jnp.concatenate([keep, other]), jnp.concatenate([other, keep])
    )
    planes = jnp.zeros((4, 2 * rows, half), BF16)
    planes = lax.dynamic_update_index_in_dim(planes, piece, zl, 0)
    for shift in (1, 7, 2):
        got = lax.ppermute(piece, ("zh", "zl"), ring(8, shift))
        planes = lax.dynamic_update_index_in_dim(planes, got, (zl + 8 - shift) % 4, 0)
    gathered = lax.all_gather(planes, ("x", "y", "c"), axis=0, tiled=False)
    return gathered.reshape(4, 4, 2, 4, 2 * rows, half)


def shards(stack, w_qkv, w_out, conv_weight, conv_bias):
    date_dev, patch_dev, width = stack.shape
    head_size = width // HEADS
    x = lax.axis_index("x")
    part = patch_dev // 4

    def cut(shift):
        block = lax.dynamic_slice_in_dim(stack, ((x + shift) % 4) * part, part, axis=1)
        block = block.reshape(date_dev, part // GROUP, GROUP, width).transpose(1, 0, 2, 3)
        return block.reshape(date_dev * part, width)

    shifts = (0, 1, 3, 2)
    own = [cut(0)] + [lax.ppermute(cut(s), "x", ring(4, s)) for s in shifts[1:]]
    partner = [lax.ppermute(block, ("zh", "zl"), ring(8, 4)) for block in own]
    w_all = gather_weights(w_qkv, w_out)
    tokens = jnp.concatenate(own + partner)
    halves, w_home = run_halves(tokens, w_all, head_size)

    whole = (4, part // GROUP, date_dev, GROUP)
    total = stack.reshape(date_dev, *whole[:2], GROUP, width).transpose(1, 2, 0, 3, 4)
    total = total.reshape(-1, width).astype(F32)
    for core in range(2):
        attended = halves[core]
        home = jnp.zeros((4, date_dev * part, width // 2), BF16)
        for slot, s in enumerate(shifts):
            back = attended[slot].reshape(date_dev * part, width // 2)
            if s:
                back = lax.ppermute(back, "x", ring(4, 4 - s))
            home = lax.dynamic_update_index_in_dim(home, back, (x + s) % 4, 0)
        if core == 0:
            home, halves[1] = tied(home, halves[1])
        columns = slice(core * width // 2, (core + 1) * width // 2)
        total += dot(home.reshape(-1, width // 2), w_home[columns])
    mixed = total.astype(BF16).reshape(*whole, width).transpose(2, 0, 1, 3, 4)

    band_rows = 2
    grid_cols = patch_dev // band_rows
    band = mixed.reshape(date_dev, band_rows, grid_cols, width)
    bands = 32
    axes = ("zl", "y", "c")
    above = lax.ppermute(band[:, -1:], axes, [(i, i + 1) for i in range(bands - 1)])
    below = lax.ppermute(band[:, :1], axes, [(i + 1, i) for i in range(bands - 1)])
    widened = jnp.concatenate([above, band, below], axis=1)
    padded = jnp.pad(widened.astype(F32), ((0, 0), (0, 0), (1, 1), (0, 0)))
    result = band.astype(F32) + conv_bias
    for row_off in range(3):
        for col_off in range(3):
            result = (
                result
                + conv_weight[row_off, col_off]
                * padded[:, row_off : row_off + band_rows, col_off : col_off + grid_cols]
            )
    return result.astype(BF16).reshape(date_dev, patch_dev, width)


def solution(mesh):
    fine = Mesh(mesh.devices.reshape(2, 4, 4, 4, 2), ("zh", "x", "zl", "y", "c"))
    date, space = ("zh", "x"), ("zl", "y", "c")
    in_specs = (P(date, space, None), P(space, None), P(space, None), P(), P())
    out_specs = P(date, space, None)
    return jax.shard_map(
        shards, mesh=fine, in_specs=in_specs, out_specs=out_specs, check_vma=False
    )
```

```python
import functools
import math

import jax
import jax.numpy as jnp
from jax import lax
from jax.experimental import pallas as pl
from jax.experimental.pallas import tpu as pltpu
from jax.sharding import Mesh
from jax.sharding import PartitionSpec as P

HEADS = 16
GROUP = 8
BF16 = jnp.bfloat16
F32 = jnp.float32


def dot(a, b):
    return jnp.dot(a, b, preferred_element_type=F32)


def attend_rows(queries, keys, values, head_size):
    width = queries.shape[1]
    rows, cols = queries.shape[0], keys.shape[0]
    scale = math.log2(math.e) / math.sqrt(head_size)
    same = (
        lax.broadcasted_iota(jnp.int32, (GROUP, cols), 0)
        == lax.broadcasted_iota(jnp.int32, (GROUP, cols), 1) % GROUP
    )
    others = jnp.where(same, 0.0, -jnp.inf)[None]
    tiles = [None] * (width // 128)
    head, heads = 0, width // head_size
    while head < heads:
        base = head * head_size // 128 * 128
        count = max(1, min((base + 256) // head_size, heads) - head)
        if base + 256 > width:
            base = width - 256
        lane = lax.broadcasted_iota(jnp.int32, (rows, 256), 1) + base
        query = queries[:, base : base + 256]
        stacked = jnp.concatenate(
            [
                jnp.where(
                    (lane >= h * head_size) & (lane < (h + 1) * head_size),
                    query,
                    jnp.zeros((), BF16),
                )
                for h in range(head, head + count)
            ]
        )
        scores = lax.dot_general(
            stacked,
            keys[:, base : base + 256],
            (((1,), (1,)), ((), ())),
            preferred_element_type=F32,
        )
        scores = (scores.reshape(-1, GROUP, cols) + others).reshape(-1, cols)
        top = jnp.max(scores, axis=1, keepdims=True)
        weights = jnp.exp2((scores - top) * scale)
        total = 1.0 / jnp.sum(weights, axis=1, keepdims=True)
        weights = weights.astype(BF16)
        out = dot(weights, values[:, base : base + 256])
        for i, h in enumerate(range(head, head + count)):
            part = slice(i * rows, (i + 1) * rows)
            for tile in range(h * head_size // 128, -(-(h + 1) * head_size // 128)):
                at = tile * 128 - base
                got = out[part, at : at + 128] * total[part]
                if tiles[tile] is None:
                    tiles[tile] = got
                else:
                    lanes = lax.broadcasted_iota(jnp.int32, (rows, 128), 1) + tile * 128
                    tiles[tile] = jnp.where(lanes < h * head_size, tiles[tile], got)
        head += count
    return jnp.concatenate(tiles, axis=1).astype(BF16)


def weight_copies(w_hbm, core, target, sem):
    half = w_hbm.shape[-1]
    return [
        pltpu.make_async_copy(
            w_hbm.at[mat, row, core],
            target.at[:, row, :, mat * half : (mat + 1) * half],
            sem.at[mat, row],
        )
        for mat in range(3)
        for row in range(4)
    ]


def attend_half(head_size, x_ref, w_ref, out, q_vm, k_vm, v_vm):
    width = x_ref.shape[1]
    half = width // 2
    own = x_ref.shape[0] // 2
    w = w_ref[...].reshape(width, 3 * half)
    got = dot(x_ref[:own], w).astype(BF16)
    q_vm[...] = got[:, :half].reshape(q_vm.shape)
    k_vm[:4] = got[:, half:width].reshape(q_vm.shape)
    v_vm[:4] = got[:, width:].reshape(q_vm.shape)
    got = dot(x_ref[own:], w[:, half:]).astype(BF16)
    k_vm[4:] = got[:, :half].reshape(q_vm.shape)
    v_vm[4:] = got[:, half:].reshape(q_vm.shape)

    def attend(group, _):
        got = attend_rows(
            q_vm[:, pl.ds(group, 1)].reshape(-1, half),
            k_vm[:, pl.ds(group, 1)].reshape(-1, half),
            v_vm[:, pl.ds(group, 1)].reshape(-1, half),
            head_size,
        )
        out[:, pl.ds(group, 1)] = got.reshape(4, 1, -1, half)
        return _

    lax.fori_loop(0, 4, attend, 0, unroll=4)


def first_kernel(head_size, x_ref, w_hbm, out, w_next, w_home, w_vm, q_vm, k_vm, v_vm, *sems):
    sem, next_sem, home_sem = sems
    half = w_hbm.shape[-1]
    now = weight_copies(w_hbm, 0, w_vm, sem)
    later = weight_copies(w_hbm, 1, w_next, next_sem)
    for core in range(2):
        for row in range(4):
            later.append(
                pltpu.make_async_copy(
                    w_hbm.at[3, row, core],
                    w_home.at[:, row, :, core * half : (core + 1) * half],
                    home_sem.at[core, row],
                )
            )
    for copy in now:
        copy.start()
    for copy in now:
        copy.wait()
    for copy in later:
        copy.start()
    attend_half(head_size, x_ref, w_vm, out, q_vm, k_vm, v_vm)
    for copy in later:
        copy.wait()


def second_kernel(head_size, x_ref, w_ref, out, q_vm, k_vm, v_vm):
    attend_half(head_size, x_ref, w_ref, out, q_vm, k_vm, v_vm)


def run_halves(x, w_all, head_size):
    rows, width = x.shape
    half, part = width // 2, rows // 32
    vmem = pl.BlockSpec(memory_space=pltpu.VMEM)
    attended = jax.ShapeDtypeStruct((4, 4, part, half), BF16)
    columns = (4, 4, width // 16, 3 * half)
    scratch = [
        pltpu.VMEM((4, 4, part, half), BF16),
        pltpu.VMEM((8, 4, part, half), BF16),
        pltpu.VMEM((8, 4, part, half), BF16),
    ]
    params = pltpu.CompilerParams(vmem_limit_bytes=36 * 1024 * 1024)
    cost = pl.CostEstimate(
        flops=5 * rows * width * half, bytes_accessed=8 * width * half, transcendentals=0
    )
    first, w_next, w_home = pl.pallas_call(
        functools.partial(first_kernel, head_size),
        out_shape=(
            attended,
            pltpu.VMEM(columns, BF16),
            jax.ShapeDtypeStruct((4, 4, width // 16, width), BF16),
        ),
        in_specs=[vmem, pl.BlockSpec(memory_space=pltpu.HBM)],
        out_specs=(vmem, vmem, vmem),
        scratch_shapes=[
            pltpu.VMEM(columns, BF16),
            *scratch,
            pltpu.SemaphoreType.DMA((3, 4)),
            pltpu.SemaphoreType.DMA((3, 4)),
            pltpu.SemaphoreType.DMA((2, 4)),
        ],
        compiler_params=params,
        cost_estimate=cost,
    )(x, w_all)
    second = pl.pallas_call(
        functools.partial(second_kernel, head_size),
        out_shape=attended,
        in_specs=[vmem, vmem],
        out_specs=vmem,
        scratch_shapes=scratch,
        compiler_params=params,
        cost_estimate=pl.CostEstimate(flops=1 << 20, bytes_accessed=1 << 12, transcendentals=0),
    )(x, w_next)
    return [first, second], w_home.reshape(width, width)


def ring(count, shift):
    return [(i, (i + shift) % count) for i in range(count)]


def tied(*values):
    return lax.optimization_barrier(values)


def gather_weights(w_qkv, w_out):
    rows, width = w_out.shape
    half = width // 2
    x, zl, core = lax.axis_index("x"), lax.axis_index("zl"), lax.axis_index("c")
    parts = [w_qkv[:, i * width : (i + 1) * width] for i in range(3)] + [w_out]
    mine = lax.select_n(x, *parts)
    keep = jnp.where(core == 0, mine[:, :half], mine[:, half:])
    give = jnp.where(core == 0, mine[:, half:], mine[:, :half])
    other = lax.ppermute(give, "c", ring(2, 1))
    piece = jnp.where(
        core == 0, jnp.concatenate([keep, other]), jnp.concatenate([other, keep])
    )
    planes = jnp.zeros((4, 2 * rows, half), BF16)
    planes = lax.dynamic_update_index_in_dim(planes, piece, zl, 0)
    for shift in (1, 7, 2):
        got = lax.ppermute(piece, ("zh", "zl"), ring(8, shift))
        planes = lax.dynamic_update_index_in_dim(planes, got, (zl + 8 - shift) % 4, 0)
    gathered = lax.all_gather(planes, ("x", "y", "c"), axis=0, tiled=False)
    return gathered.reshape(4, 4, 2, 4, 2 * rows, half)


def shards(stack, w_qkv, w_out, conv_weight, conv_bias):
    date_dev, patch_dev, width = stack.shape
    head_size = width // HEADS
    x = lax.axis_index("x")
    part = patch_dev // 4

    def cut(shift):
        block = lax.dynamic_slice_in_dim(stack, ((x + shift) % 4) * part, part, axis=1)
        block = block.reshape(date_dev, part // GROUP, GROUP, width).transpose(1, 0, 2, 3)
        return block.reshape(date_dev * part, width)

    shifts = (0, 1, 3, 2)
    own = [cut(0)] + [lax.ppermute(cut(s), "x", ring(4, s)) for s in shifts[1:]]
    partner = [lax.ppermute(block, ("zh", "zl"), ring(8, 4)) for block in own]
    w_all = gather_weights(w_qkv, w_out)
    tokens = jnp.concatenate(own + partner)
    halves, w_home = run_halves(tokens, w_all, head_size)

    whole = (4, part // GROUP, date_dev, GROUP)
    total = stack.reshape(date_dev, *whole[:2], GROUP, width).transpose(1, 2, 0, 3, 4)
    total = total.reshape(-1, width).astype(F32)
    for core in range(2):
        attended = halves[core]
        home = jnp.zeros((4, date_dev * part, width // 2), BF16)
        for slot, s in enumerate(shifts):
            back = attended[slot].reshape(date_dev * part, width // 2)
            if s:
                back = lax.ppermute(back, "x", ring(4, 4 - s))
            home = lax.dynamic_update_index_in_dim(home, back, (x + s) % 4, 0)
        if core == 0:
            home, halves[1] = tied(home, halves[1])
        columns = slice(core * width // 2, (core + 1) * width // 2)
        total += dot(home.reshape(-1, width // 2), w_home[columns])
    mixed = total.astype(BF16).reshape(*whole, width).transpose(2, 0, 1, 3, 4)

    band_rows = 2
    grid_cols = patch_dev // band_rows
    band = mixed.reshape(date_dev, band_rows, grid_cols, width)
    bands = 32
    axes = ("zl", "y", "c")
    above = lax.ppermute(band[:, -1:], axes, [(i, i + 1) for i in range(bands - 1)])
    below = lax.ppermute(band[:, :1], axes, [(i + 1, i) for i in range(bands - 1)])
    widened = jnp.concatenate([above, band, below], axis=1)
    padded = jnp.pad(widened.astype(F32), ((0, 0), (0, 0), (1, 1), (0, 0)))
    result = band.astype(F32) + conv_bias
    for row_off in range(3):
        for col_off in range(3):
            result = (
                result
                + conv_weight[row_off, col_off]
                * padded[:, row_off : row_off + band_rows, col_off : col_off + grid_cols]
            )
    return result.astype(BF16).reshape(date_dev, patch_dev, width)


def solution(mesh):
    fine = Mesh(mesh.devices.reshape(2, 4, 4, 4, 2), ("zh", "x", "zl", "y", "c"))
    date, space = ("zh", "x"), ("zl", "y", "c")
    in_specs = (P(date, space, None), P(space, None), P(space, None), P(), P())
    out_specs = P(date, space, None)
    return jax.shard_map(
        shards, mesh=fine, in_specs=in_specs, out_specs=out_specs, check_vma=False
    )
```

```python
import functools
import math

import jax
import jax.numpy as jnp
from jax import lax
from jax.experimental import pallas as pl
from jax.experimental.pallas import tpu as pltpu
from jax.sharding import Mesh
from jax.sharding import PartitionSpec as P

HEADS = 16
GROUP = 8
BF16 = jnp.bfloat16
F32 = jnp.float32


def dot(a, b):
    return jnp.dot(a, b, preferred_element_type=F32)


def attend_rows(queries, keys, values, head_size):
    width = queries.shape[1]
    rows, cols = queries.shape[0], keys.shape[0]
    scale = math.log2(math.e) / math.sqrt(head_size)
    same = (
        lax.broadcasted_iota(jnp.int32, (GROUP, cols), 0)
        == lax.broadcasted_iota(jnp.int32, (GROUP, cols), 1) % GROUP
    )
    others = jnp.where(same, 0.0, -jnp.inf)[None]
    tiles = [None] * (width // 128)
    head, heads = 0, width // head_size
    while head < heads:
        base = head * head_size // 128 * 128
        count = max(1, min((base + 256) // head_size, heads) - head)
        if base + 256 > width:
            base = width - 256
        lane = lax.broadcasted_iota(jnp.int32, (rows, 256), 1) + base
        query = queries[:, base : base + 256]
        stacked = jnp.concatenate(
            [
                jnp.where(
                    (lane >= h * head_size) & (lane < (h + 1) * head_size),
                    query,
                    jnp.zeros((), BF16),
                )
                for h in range(head, head + count)
            ]
        )
        scores = lax.dot_general(
            stacked,
            keys[:, base : base + 256],
            (((1,), (1,)), ((), ())),
            preferred_element_type=F32,
        )
        scores = (scores.reshape(-1, GROUP, cols) + others).reshape(-1, cols)
        top = jnp.max(scores, axis=1, keepdims=True)
        weights = jnp.exp2((scores - top) * scale)
        total = 1.0 / jnp.sum(weights, axis=1, keepdims=True)
        weights = weights.astype(BF16)
        out = dot(weights, values[:, base : base + 256])
        for i, h in enumerate(range(head, head + count)):
            part = slice(i * rows, (i + 1) * rows)
            for tile in range(h * head_size // 128, -(-(h + 1) * head_size // 128)):
                at = tile * 128 - base
                got = out[part, at : at + 128] * total[part]
                if tiles[tile] is None:
                    tiles[tile] = got
                else:
                    lanes = lax.broadcasted_iota(jnp.int32, (rows, 128), 1) + tile * 128
                    tiles[tile] = jnp.where(lanes < h * head_size, tiles[tile], got)
        head += count
    return jnp.concatenate(tiles, axis=1).astype(BF16)


def weight_copies(w_hbm, core, target, sem):
    half = w_hbm.shape[-1]
    return [
        pltpu.make_async_copy(
            w_hbm.at[mat, row, core],
            target.at[:, row, :, mat * half : (mat + 1) * half],
            sem.at[mat, row],
        )
        for mat in range(3)
        for row in range(4)
    ]


def attend_half(head_size, x_ref, w_ref, out, q_vm, k_vm, v_vm):
    width = x_ref.shape[1]
    half = width // 2
    own = x_ref.shape[0] // 2
    w = w_ref[...].reshape(width, 3 * half)
    got = dot(x_ref[:own], w).astype(BF16)
    q_vm[...] = got[:, :half].reshape(q_vm.shape)
    k_vm[:4] = got[:, half:width].reshape(q_vm.shape)
    v_vm[:4] = got[:, width:].reshape(q_vm.shape)
    got = dot(x_ref[own:], w[:, half:]).astype(BF16)
    k_vm[4:] = got[:, :half].reshape(q_vm.shape)
    v_vm[4:] = got[:, half:].reshape(q_vm.shape)

    def attend(group, _):
        got = attend_rows(
            q_vm[:, pl.ds(group, 1)].reshape(-1, half),
            k_vm[:, pl.ds(group, 1)].reshape(-1, half),
            v_vm[:, pl.ds(group, 1)].reshape(-1, half),
            head_size,
        )
        out[:, pl.ds(group, 1)] = got.reshape(4, 1, -1, half)
        return _

    lax.fori_loop(0, 4, attend, 0, unroll=4)


def first_kernel(head_size, x_ref, w_hbm, out, w_next, w_home, w_vm, q_vm, k_vm, v_vm, *sems):
    sem, next_sem, home_sem = sems
    half = w_hbm.shape[-1]
    now = weight_copies(w_hbm, 0, w_vm, sem)
    later = weight_copies(w_hbm, 1, w_next, next_sem)
    for core in range(2):
        for row in range(4):
            later.append(
                pltpu.make_async_copy(
                    w_hbm.at[3, row, core],
                    w_home.at[:, row, :, core * half : (core + 1) * half],
                    home_sem.at[core, row],
                )
            )
    for copy in now:
        copy.start()
    for copy in now:
        copy.wait()
    for copy in later:
        copy.start()
    attend_half(head_size, x_ref, w_vm, out, q_vm, k_vm, v_vm)
    for copy in later:
        copy.wait()


def second_kernel(head_size, x_ref, w_ref, out, q_vm, k_vm, v_vm):
    attend_half(head_size, x_ref, w_ref, out, q_vm, k_vm, v_vm)


def run_halves(x, w_all, head_size):
    rows, width = x.shape
    half, part = width // 2, rows // 32
    vmem = pl.BlockSpec(memory_space=pltpu.VMEM)
    attended = jax.ShapeDtypeStruct((4, 4, part, half), BF16)
    columns = (4, 4, width // 16, 3 * half)
    scratch = [
        pltpu.VMEM((4, 4, part, half), BF16),
        pltpu.VMEM((8, 4, part, half), BF16),
        pltpu.VMEM((8, 4, part, half), BF16),
    ]
    params = pltpu.CompilerParams(vmem_limit_bytes=36 * 1024 * 1024)
    cost = pl.CostEstimate(
        flops=5 * rows * width * half, bytes_accessed=8 * width * half, transcendentals=0
    )
    first, w_next, w_home = pl.pallas_call(
        functools.partial(first_kernel, head_size),
        out_shape=(
            attended,
            pltpu.VMEM(columns, BF16),
            jax.ShapeDtypeStruct((4, 4, width // 16, width), BF16),
        ),
        in_specs=[vmem, pl.BlockSpec(memory_space=pltpu.HBM)],
        out_specs=(vmem, vmem, vmem),
        scratch_shapes=[
            pltpu.VMEM(columns, BF16),
            *scratch,
            pltpu.SemaphoreType.DMA((3, 4)),
            pltpu.SemaphoreType.DMA((3, 4)),
            pltpu.SemaphoreType.DMA((2, 4)),
        ],
        compiler_params=params,
        cost_estimate=cost,
    )(x, w_all)
    second = pl.pallas_call(
        functools.partial(second_kernel, head_size),
        out_shape=attended,
        in_specs=[vmem, vmem],
        out_specs=vmem,
        scratch_shapes=scratch,
        compiler_params=params,
        cost_estimate=pl.CostEstimate(flops=1 << 20, bytes_accessed=1 << 12, transcendentals=0),
    )(x, w_next)
    return [first, second], w_home.reshape(width, width)


def ring(count, shift):
    return [(i, (i + shift) % count) for i in range(count)]


def pairs(count, mask):
    return [(i, i ^ mask) for i in range(count)]


def tied(*values):
    return lax.optimization_barrier(values)


def gather_weights(w_qkv, w_out):
    rows, width = w_out.shape
    half = width // 2
    x, zl, core = lax.axis_index("x"), lax.axis_index("zl"), lax.axis_index("c")
    parts = [w_qkv[:, i * width : (i + 1) * width] for i in range(3)] + [w_out]
    mine = lax.select_n(x, *parts)
    keep = jnp.where(core == 0, mine[:, :half], mine[:, half:])
    give = jnp.where(core == 0, mine[:, half:], mine[:, :half])
    other = lax.ppermute(give, "c", ring(2, 1))
    piece = jnp.where(
        core == 0, jnp.concatenate([keep, other]), jnp.concatenate([other, keep])
    )
    planes = jnp.zeros((4, 2 * rows, half), BF16)
    planes = lax.dynamic_update_index_in_dim(planes, piece, zl, 0)
    below = [(z, (z + 7) % 8 if z % 2 == 0 else (z + 1) % 8) for z in range(8)]
    for moves, source in (
        (pairs(8, 1), zl ^ 1),
        (below, jnp.where(zl % 2 == 0, zl + 3, zl + 1) % 4),
        (pairs(8, 2), zl ^ 2),
    ):
        got = lax.ppermute(piece, ("zh", "zl"), moves)
        planes = lax.dynamic_update_index_in_dim(planes, got, source, 0)
    gathered = lax.all_gather(planes, ("x", "y", "c"), axis=0, tiled=False)
    return gathered.reshape(4, 4, 2, 4, 2 * rows, half)


def shards(stack, w_qkv, w_out, conv_weight, conv_bias):
    date_dev, patch_dev, width = stack.shape
    head_size = width // HEADS
    x = lax.axis_index("x")
    part = patch_dev // 4

    def cut(mask):
        block = lax.dynamic_slice_in_dim(stack, (x ^ mask) * part, part, axis=1)
        block = block.reshape(date_dev, part // GROUP, GROUP, width).transpose(1, 0, 2, 3)
        return block.reshape(date_dev * part, width)

    masks = (0, 1, 3, 2)
    own = [cut(0)] + [lax.ppermute(cut(m), "x", pairs(4, m)) for m in masks[1:]]
    partner = [lax.ppermute(block, ("zh", "zl"), ring(8, 4)) for block in own]
    w_all = gather_weights(w_qkv, w_out)
    tokens = jnp.concatenate(own + partner)
    halves, w_home = run_halves(tokens, w_all, head_size)

    whole = (4, part // GROUP, date_dev, GROUP)
    total = stack.reshape(date_dev, *whole[:2], GROUP, width).transpose(1, 2, 0, 3, 4)
    total = total.reshape(-1, width).astype(F32)
    for core in range(2):
        attended = halves[core]
        home = jnp.zeros((4, date_dev * part, width // 2), BF16)
        for slot, m in enumerate(masks):
            back = attended[slot].reshape(date_dev * part, width // 2)
            if m:
                back = lax.ppermute(back, "x", pairs(4, m))
            home = lax.dynamic_update_index_in_dim(home, back, x ^ m, 0)
        if core == 0:
            home, halves[1] = tied(home, halves[1])
        columns = slice(core * width // 2, (core + 1) * width // 2)
        total += dot(home.reshape(-1, width // 2), w_home[columns])
    mixed = total.astype(BF16).reshape(*whole, width).transpose(2, 0, 1, 3, 4)

    band_rows = 2
    grid_cols = patch_dev // band_rows
    band = mixed.reshape(date_dev, band_rows, grid_cols, width)
    axes = ("zl", "y", "c")
    core = lax.axis_index("c")
    first, last = band[:, :1], band[:, -1:]
    near = lax.ppermute(jnp.where(core == 0, last, first), "c", pairs(2, 1))
    across = [(i, i + 1 if i % 2 else i - 1) for i in range(1, 31)]
    far = lax.ppermute(jnp.where(core == 0, first, last), axes, across)
    above, below = jnp.where(core == 0, far, near), jnp.where(core == 0, near, far)
    widened = jnp.concatenate([above, band, below], axis=1)
    padded = jnp.pad(widened.astype(F32), ((0, 0), (0, 0), (1, 1), (0, 0)))
    result = band.astype(F32) + conv_bias
    for row_off in range(3):
        for col_off in range(3):
            result = (
                result
                + conv_weight[row_off, col_off]
                * padded[:, row_off : row_off + band_rows, col_off : col_off + grid_cols]
            )
    return result.astype(BF16).reshape(date_dev, patch_dev, width)


def solution(mesh):
    fine = Mesh(mesh.devices.reshape(2, 4, 4, 4, 2), ("zh", "x", "zl", "y", "c"))
    date, space = ("zh", "x"), ("zl", "y", "c")
    in_specs = (P(date, space, None), P(space, None), P(space, None), P(), P())
    out_specs = P(date, space, None)
    return jax.shard_map(
        shards, mesh=fine, in_specs=in_specs, out_specs=out_specs, check_vma=False
    )
```

```python
import functools
import math

import jax
import jax.numpy as jnp
from jax import lax
from jax.experimental import pallas as pl
from jax.experimental.pallas import tpu as pltpu
from jax.sharding import Mesh
from jax.sharding import PartitionSpec as P

HEADS = 16
GROUP = 8
BF16 = jnp.bfloat16
F32 = jnp.float32


def dot(a, b):
    return jnp.dot(a, b, preferred_element_type=F32)


def attend_rows(queries, keys, values, head_size):
    width = queries.shape[1]
    rows, cols = queries.shape[0], keys.shape[0]
    scale = math.log2(math.e) / math.sqrt(head_size)
    same = (
        lax.broadcasted_iota(jnp.int32, (GROUP, cols), 0)
        == lax.broadcasted_iota(jnp.int32, (GROUP, cols), 1) % GROUP
    )
    others = jnp.where(same, 0.0, -jnp.inf)[None]
    tiles = [None] * (width // 128)
    head, heads = 0, width // head_size
    while head < heads:
        base = head * head_size // 128 * 128
        count = max(1, min((base + 256) // head_size, heads) - head)
        if base + 256 > width:
            base = width - 256
        lane = lax.broadcasted_iota(jnp.int32, (rows, 256), 1) + base
        query = queries[:, base : base + 256]
        stacked = jnp.concatenate(
            [
                jnp.where(
                    (lane >= h * head_size) & (lane < (h + 1) * head_size),
                    query,
                    jnp.zeros((), BF16),
                )
                for h in range(head, head + count)
            ]
        )
        scores = lax.dot_general(
            stacked,
            keys[:, base : base + 256],
            (((1,), (1,)), ((), ())),
            preferred_element_type=F32,
        )
        scores = (scores.reshape(-1, GROUP, cols) + others).reshape(-1, cols)
        top = jnp.max(scores, axis=1, keepdims=True)
        weights = jnp.exp2((scores - top) * scale)
        total = 1.0 / jnp.sum(weights, axis=1, keepdims=True)
        weights = weights.astype(BF16)
        out = dot(weights, values[:, base : base + 256])
        for i, h in enumerate(range(head, head + count)):
            part = slice(i * rows, (i + 1) * rows)
            for tile in range(h * head_size // 128, -(-(h + 1) * head_size // 128)):
                at = tile * 128 - base
                got = out[part, at : at + 128] * total[part]
                if tiles[tile] is None:
                    tiles[tile] = got
                else:
                    lanes = lax.broadcasted_iota(jnp.int32, (rows, 128), 1) + tile * 128
                    tiles[tile] = jnp.where(lanes < h * head_size, tiles[tile], got)
        head += count
    return jnp.concatenate(tiles, axis=1).astype(BF16)


def weight_copies(w_hbm, core, target, sem):
    half = w_hbm.shape[-1]
    return [
        pltpu.make_async_copy(
            w_hbm.at[mat, row, core],
            target.at[:, row, :, mat * half : (mat + 1) * half],
            sem.at[mat, row],
        )
        for mat in range(3)
        for row in range(4)
    ]


def attend_half(head_size, x_ref, w_ref, out, q_vm, k_vm, v_vm, ready=lambda mat: None):
    width = x_ref.shape[1]
    half = width // 2
    own = x_ref.shape[0] // 2
    ready(0)
    q_vm[...] = dot(x_ref[:own], w_ref[..., :half].reshape(width, half)).astype(BF16).reshape(
        q_vm.shape
    )
    ready(1)
    ready(2)
    got = dot(x_ref[...], w_ref[..., half:].reshape(width, width)).astype(BF16)
    k_vm[...] = got[:, :half].reshape(k_vm.shape)
    v_vm[...] = got[:, half:].reshape(v_vm.shape)

    def attend(group, _):
        got = attend_rows(
            q_vm[:, pl.ds(group, 1)].reshape(-1, half),
            k_vm[:, pl.ds(group, 1)].reshape(-1, half),
            v_vm[:, pl.ds(group, 1)].reshape(-1, half),
            head_size,
        )
        out[:, pl.ds(group, 1)] = got.reshape(4, 1, -1, half)
        return _

    lax.fori_loop(0, 4, attend, 0, unroll=4)


def first_kernel(head_size, x_ref, w_hbm, out, w_next, w_home, w_vm, q_vm, k_vm, v_vm, *sems):
    sem, next_sem, home_sem = sems
    half = w_hbm.shape[-1]
    now = weight_copies(w_hbm, 0, w_vm, sem)
    later = weight_copies(w_hbm, 1, w_next, next_sem)
    for core in range(2):
        for row in range(4):
            later.append(
                pltpu.make_async_copy(
                    w_hbm.at[3, row, core],
                    w_home.at[:, row, :, core * half : (core + 1) * half],
                    home_sem.at[core, row],
                )
            )
    for copy in now:
        copy.start()

    def ready(mat):
        for copy in now[4 * mat : 4 * mat + 4]:
            copy.wait()
        if mat == 2:
            for copy in later:
                copy.start()

    attend_half(head_size, x_ref, w_vm, out, q_vm, k_vm, v_vm, ready)
    for copy in later:
        copy.wait()


def second_kernel(head_size, x_ref, w_ref, out, q_vm, k_vm, v_vm):
    attend_half(head_size, x_ref, w_ref, out, q_vm, k_vm, v_vm)


def run_halves(x, w_all, head_size):
    rows, width = x.shape
    half, part = width // 2, rows // 32
    vmem = pl.BlockSpec(memory_space=pltpu.VMEM)
    attended = jax.ShapeDtypeStruct((4, 4, part, half), BF16)
    columns = (4, 4, width // 16, 3 * half)
    scratch = [
        pltpu.VMEM((4, 4, part, half), BF16),
        pltpu.VMEM((8, 4, part, half), BF16),
        pltpu.VMEM((8, 4, part, half), BF16),
    ]
    params = pltpu.CompilerParams(vmem_limit_bytes=36 * 1024 * 1024)
    cost = pl.CostEstimate(
        flops=5 * rows * width * half, bytes_accessed=8 * width * half, transcendentals=0
    )
    first, w_next, w_home = pl.pallas_call(
        functools.partial(first_kernel, head_size),
        out_shape=(
            attended,
            pltpu.VMEM(columns, BF16),
            jax.ShapeDtypeStruct((4, 4, width // 16, width), BF16),
        ),
        in_specs=[vmem, pl.BlockSpec(memory_space=pltpu.HBM)],
        out_specs=(vmem, vmem, vmem),
        scratch_shapes=[
            pltpu.VMEM(columns, BF16),
            *scratch,
            pltpu.SemaphoreType.DMA((3, 4)),
            pltpu.SemaphoreType.DMA((3, 4)),
            pltpu.SemaphoreType.DMA((2, 4)),
        ],
        compiler_params=params,
        cost_estimate=cost,
    )(x, w_all)
    second = pl.pallas_call(
        functools.partial(second_kernel, head_size),
        out_shape=attended,
        in_specs=[vmem, vmem],
        out_specs=vmem,
        scratch_shapes=scratch,
        compiler_params=params,
        cost_estimate=pl.CostEstimate(flops=1 << 20, bytes_accessed=1 << 12, transcendentals=0),
    )(x, w_next)
    return [first, second], w_home.reshape(width, width)


def ring(count, shift):
    return [(i, (i + shift) % count) for i in range(count)]


def pairs(count, mask):
    return [(i, i ^ mask) for i in range(count)]


def tied(*values):
    return lax.optimization_barrier(values)


def gather_weights(w_qkv, w_out):
    rows, width = w_out.shape
    half = width // 2
    x, zl, core = lax.axis_index("x"), lax.axis_index("zl"), lax.axis_index("c")
    parts = [w_qkv[:, i * width : (i + 1) * width] for i in range(3)] + [w_out]
    mine = lax.select_n(x, *parts)
    keep = jnp.where(core == 0, mine[:, :half], mine[:, half:])
    give = jnp.where(core == 0, mine[:, half:], mine[:, :half])
    other = lax.ppermute(give, "c", ring(2, 1))
    piece = jnp.where(
        core == 0, jnp.concatenate([keep, other]), jnp.concatenate([other, keep])
    )
    planes = jnp.zeros((4, 2 * rows, half), BF16)
    planes = lax.dynamic_update_index_in_dim(planes, piece, zl, 0)
    below = [(z, (z + 7) % 8 if z % 2 == 0 else (z + 1) % 8) for z in range(8)]
    for moves, source in (
        (pairs(8, 1), zl ^ 1),
        (below, jnp.where(zl % 2 == 0, zl + 3, zl + 1) % 4),
        (pairs(8, 2), zl ^ 2),
    ):
        got = lax.ppermute(piece, ("zh", "zl"), moves)
        planes = lax.dynamic_update_index_in_dim(planes, got, source, 0)
    gathered = lax.all_gather(planes, ("x", "y", "c"), axis=0, tiled=False)
    return gathered.reshape(4, 4, 2, 4, 2 * rows, half)


def shards(stack, w_qkv, w_out, conv_weight, conv_bias):
    date_dev, patch_dev, width = stack.shape
    head_size = width // HEADS
    x = lax.axis_index("x")
    part = patch_dev // 4

    def cut(mask):
        block = lax.dynamic_slice_in_dim(stack, (x ^ mask) * part, part, axis=1)
        block = block.reshape(date_dev, part // GROUP, GROUP, width).transpose(1, 0, 2, 3)
        return block.reshape(date_dev * part, width)

    masks = (0, 1, 3, 2)
    own = [cut(0)] + [lax.ppermute(cut(m), "x", pairs(4, m)) for m in masks[1:]]
    partner = [lax.ppermute(block, ("zh", "zl"), ring(8, 4)) for block in own]
    w_all = gather_weights(w_qkv, w_out)
    tokens = jnp.concatenate(own + partner)
    halves, w_home = run_halves(tokens, w_all, head_size)

    whole = (4, part // GROUP, date_dev, GROUP)
    total = stack.reshape(date_dev, *whole[:2], GROUP, width).transpose(1, 2, 0, 3, 4)
    total = total.reshape(-1, width).astype(F32)
    for core in range(2):
        attended = halves[core]
        home = jnp.zeros((4, date_dev * part, width // 2), BF16)
        for slot, m in enumerate(masks):
            back = attended[slot].reshape(date_dev * part, width // 2)
            if m:
                back = lax.ppermute(back, "x", pairs(4, m))
            home = lax.dynamic_update_index_in_dim(home, back, x ^ m, 0)
        if core == 0:
            home, halves[1] = tied(home, halves[1])
        columns = slice(core * width // 2, (core + 1) * width // 2)
        total += dot(home.reshape(-1, width // 2), w_home[columns])
    mixed = total.astype(BF16).reshape(*whole, width).transpose(2, 0, 1, 3, 4)

    band_rows = 2
    grid_cols = patch_dev // band_rows
    band = mixed.reshape(date_dev, band_rows, grid_cols, width)
    axes = ("zl", "y", "c")
    core = lax.axis_index("c")
    first, last = band[:, :1], band[:, -1:]
    near = lax.ppermute(jnp.where(core == 0, last, first), "c", pairs(2, 1))
    across = [(i, i + 1 if i % 2 else i - 1) for i in range(1, 31)]
    far = lax.ppermute(jnp.where(core == 0, first, last), axes, across)
    above, below = jnp.where(core == 0, far, near), jnp.where(core == 0, near, far)
    halo = jnp.concatenate([above, below], axis=1)

    def taps(rows, weights):
        padded = jnp.pad(rows.astype(F32), ((0, 0), (0, 0), (1, 1), (0, 0)))
        return sum(weights[:, i, None] * padded[:, :, i : i + grid_cols] for i in range(3))

    result = band.astype(F32) + conv_bias
    result += taps(band, conv_weight[1:2])
    result += taps(band[:, ::-1], jnp.stack([conv_weight[2], conv_weight[0]]))
    result, halo = tied(result, halo)
    result += taps(halo, jnp.stack([conv_weight[0], conv_weight[2]]))
    return result.astype(BF16).reshape(date_dev, patch_dev, width)


def solution(mesh):
    fine = Mesh(mesh.devices.reshape(2, 4, 4, 4, 2), ("zh", "x", "zl", "y", "c"))
    date, space = ("zh", "x"), ("zl", "y", "c")
    in_specs = (P(date, space, None), P(space, None), P(space, None), P(), P())
    out_specs = P(date, space, None)
    return jax.shard_map(
        shards, mesh=fine, in_specs=in_specs, out_specs=out_specs, check_vma=False
    )
```

```python
import functools
import math

import jax
import jax.numpy as jnp
from jax import lax
from jax.experimental import pallas as pl
from jax.experimental.pallas import tpu as pltpu
from jax.sharding import Mesh
from jax.sharding import PartitionSpec as P

HEADS = 16
GROUP = 8
BF16 = jnp.bfloat16
F32 = jnp.float32


def dot(a, b):
    return jnp.dot(a, b, preferred_element_type=F32)


def attend_rows(queries, keys, values, head_size):
    width = queries.shape[1]
    rows, cols = queries.shape[0], keys.shape[0]
    scale = math.log2(math.e) / math.sqrt(head_size)
    same = (
        lax.broadcasted_iota(jnp.int32, (GROUP, cols), 0)
        == lax.broadcasted_iota(jnp.int32, (GROUP, cols), 1) % GROUP
    )
    others = jnp.where(same, 0.0, -jnp.inf)[None]
    windows, head, heads = [], 0, width // head_size
    while head < heads:
        count = max(1, min((head * head_size // 128 * 128 + 256) // head_size, heads) - head)
        windows.append((min(head * head_size // 128 * 128, width - 256), range(head, head + count)))
        head += count

    def score(base, members):
        lane = lax.broadcasted_iota(jnp.int32, (rows, 256), 1) + base
        query = queries[:, base : base + 256]
        stacked = jnp.concatenate(
            [
                jnp.where(
                    (lane >= h * head_size) & (lane < (h + 1) * head_size),
                    query,
                    jnp.zeros((), BF16),
                )
                for h in members
            ]
        )
        scores = lax.dot_general(
            stacked,
            keys[:, base : base + 256],
            (((1,), (1,)), ((), ())),
            preferred_element_type=F32,
        )
        return (scores.reshape(-1, GROUP, cols) + others).reshape(-1, cols)

    tiles = [None] * (width // 128)

    def gather(base, members, scores):
        top = jnp.max(scores, axis=1, keepdims=True)
        weights = jnp.exp2((scores - top) * scale)
        total = 1.0 / jnp.sum(weights, axis=1, keepdims=True)
        out = dot(weights.astype(BF16), values[:, base : base + 256])
        for i, h in enumerate(members):
            part = slice(i * rows, (i + 1) * rows)
            for tile in range(h * head_size // 128, -(-(h + 1) * head_size // 128)):
                at = tile * 128 - base
                got = out[part, at : at + 128] * total[part]
                if tiles[tile] is None:
                    tiles[tile] = got
                else:
                    lanes = lax.broadcasted_iota(jnp.int32, (rows, 128), 1) + tile * 128
                    tiles[tile] = jnp.where(lanes < h * head_size, tiles[tile], got)

    all_scores = [score(*window) for window in windows]
    for window, scores in zip(windows, all_scores):
        gather(*window, scores)
    return jnp.concatenate(tiles, axis=1).astype(BF16)


def weight_copies(w_hbm, core, target, sem):
    half = w_hbm.shape[-1]
    return [
        pltpu.make_async_copy(
            w_hbm.at[mat, row, core],
            target.at[:, row, :, mat * half : (mat + 1) * half],
            sem.at[mat, row],
        )
        for mat in range(3)
        for row in range(4)
    ]


def attend_half(head_size, x_ref, w_ref, out, ready=lambda mat: None):
    width = x_ref.shape[1]
    half = width // 2
    part = out.shape[2]
    turns = 4
    take = 4 // turns

    def project(turn):
        x = x_ref[...].reshape(8, 4, part, width)[:, turn * take : (turn + 1) * take]
        x = x.reshape(8 * take * part, width)
        q = dot(x[: 4 * take * part], w_ref[..., :half].reshape(width, half)).astype(BF16)
        if turn == 0:
            ready(1)
            ready(2)
        kv = dot(x, w_ref[..., half:].reshape(width, width)).astype(BF16)
        shape = (8, take, part, half)
        return q.reshape(4, *shape[1:]), kv[:, :half].reshape(shape), kv[:, half:].reshape(shape)

    def attend(turn, q, k, v):
        for i in range(take):
            got = attend_rows(*(m[:, i].reshape(-1, half) for m in (q, k, v)), head_size)
            out[:, turn * take + i] = got.reshape(4, -1, half)

    ready(0)
    held = project(0)
    for turn in range(turns):
        after = project(turn + 1) if turn + 1 < turns else None
        attend(turn, *held)
        held = after


def first_kernel(head_size, x_ref, w_hbm, out, w_next, w_home, w_vm, *sems):
    sem, next_sem, home_sem = sems
    half = w_hbm.shape[-1]
    now = weight_copies(w_hbm, 0, w_vm, sem)
    later = weight_copies(w_hbm, 1, w_next, next_sem)
    for core in range(2):
        for row in range(4):
            later.append(
                pltpu.make_async_copy(
                    w_hbm.at[3, row, core],
                    w_home.at[:, row, :, core * half : (core + 1) * half],
                    home_sem.at[core, row],
                )
            )
    for copy in now:
        copy.start()

    def ready(mat):
        for copy in now[4 * mat : 4 * mat + 4]:
            copy.wait()
        if mat == 2:
            for copy in later:
                copy.start()

    attend_half(head_size, x_ref, w_vm, out, ready)
    for copy in later:
        copy.wait()


def second_kernel(head_size, x_ref, w_ref, out):
    attend_half(head_size, x_ref, w_ref, out)


def run_halves(x, w_all, head_size):
    rows, width = x.shape
    half, part = width // 2, rows // 32
    vmem = pl.BlockSpec(memory_space=pltpu.VMEM)
    attended = jax.ShapeDtypeStruct((4, 4, part, half), BF16)
    columns = (4, 4, width // 16, 3 * half)
    params = pltpu.CompilerParams(vmem_limit_bytes=36 * 1024 * 1024)
    cost = pl.CostEstimate(
        flops=5 * rows * width * half, bytes_accessed=8 * width * half, transcendentals=0
    )
    first, w_next, w_home = pl.pallas_call(
        functools.partial(first_kernel, head_size),
        out_shape=(
            attended,
            pltpu.VMEM(columns, BF16),
            jax.ShapeDtypeStruct((4, 4, width // 16, width), BF16),
        ),
        in_specs=[vmem, pl.BlockSpec(memory_space=pltpu.HBM)],
        out_specs=(vmem, vmem, vmem),
        scratch_shapes=[
            pltpu.VMEM(columns, BF16),
            pltpu.SemaphoreType.DMA((3, 4)),
            pltpu.SemaphoreType.DMA((3, 4)),
            pltpu.SemaphoreType.DMA((2, 4)),
        ],
        compiler_params=params,
        cost_estimate=cost,
    )(x, w_all)
    second = pl.pallas_call(
        functools.partial(second_kernel, head_size),
        out_shape=attended,
        in_specs=[vmem, vmem],
        out_specs=vmem,
        compiler_params=params,
        cost_estimate=pl.CostEstimate(flops=1 << 20, bytes_accessed=1 << 12, transcendentals=0),
    )(x, w_next)
    return [first, second], w_home.reshape(width, width)


def ring(count, shift):
    return [(i, (i + shift) % count) for i in range(count)]


def pairs(count, mask):
    return [(i, i ^ mask) for i in range(count)]


def tied(*values):
    return lax.optimization_barrier(values)


def gather_weights(w_qkv, w_out):
    rows, width = w_out.shape
    half = width // 2
    x, zl, core = lax.axis_index("x"), lax.axis_index("zl"), lax.axis_index("c")
    parts = [w_qkv[:, i * width : (i + 1) * width] for i in range(3)] + [w_out]
    mine = lax.select_n(x, *parts)
    keep = jnp.where(core == 0, mine[:, :half], mine[:, half:])
    give = jnp.where(core == 0, mine[:, half:], mine[:, :half])
    other = lax.ppermute(give, "c", ring(2, 1))
    piece = jnp.where(
        core == 0, jnp.concatenate([keep, other]), jnp.concatenate([other, keep])
    )
    planes = jnp.zeros((4, 2 * rows, half), BF16)
    planes = lax.dynamic_update_index_in_dim(planes, piece, zl, 0)
    below = [(z, (z + 7) % 8 if z % 2 == 0 else (z + 1) % 8) for z in range(8)]
    for moves, source in (
        (pairs(8, 1), zl ^ 1),
        (below, jnp.where(zl % 2 == 0, zl + 3, zl + 1) % 4),
        (pairs(8, 2), zl ^ 2),
    ):
        got = lax.ppermute(piece, ("zh", "zl"), moves)
        planes = lax.dynamic_update_index_in_dim(planes, got, source, 0)
    gathered = lax.all_gather(planes, ("x", "y", "c"), axis=0, tiled=False)
    return gathered.reshape(4, 4, 2, 4, 2 * rows, half)


def shards(stack, w_qkv, w_out, conv_weight, conv_bias):
    date_dev, patch_dev, width = stack.shape
    head_size = width // HEADS
    x = lax.axis_index("x")
    part = patch_dev // 4

    def cut(mask):
        block = lax.dynamic_slice_in_dim(stack, (x ^ mask) * part, part, axis=1)
        block = block.reshape(date_dev, part // GROUP, GROUP, width).transpose(1, 0, 2, 3)
        return block.reshape(date_dev * part, width)

    masks = (0, 1, 3, 2)
    own = [cut(0)] + [lax.ppermute(cut(m), "x", pairs(4, m)) for m in masks[1:]]
    partner = [lax.ppermute(block, ("zh", "zl"), ring(8, 4)) for block in own]
    w_all = gather_weights(w_qkv, w_out)
    tokens = jnp.concatenate(own + partner)
    halves, w_home = run_halves(tokens, w_all, head_size)

    whole = (4, part // GROUP, date_dev, GROUP)
    total = stack.reshape(date_dev, *whole[:2], GROUP, width).transpose(1, 2, 0, 3, 4)
    total = total.reshape(-1, width).astype(F32)
    for core in range(2):
        attended = halves[core]
        home = jnp.zeros((4, date_dev * part, width // 2), BF16)
        for slot, m in enumerate(masks):
            back = attended[slot].reshape(date_dev * part, width // 2)
            if m:
                back = lax.ppermute(back, "x", pairs(4, m))
            home = lax.dynamic_update_index_in_dim(home, back, x ^ m, 0)
        if core == 0:
            home, halves[1] = tied(home, halves[1])
        columns = slice(core * width // 2, (core + 1) * width // 2)
        total += dot(home.reshape(-1, width // 2), w_home[columns])
    mixed = total.astype(BF16).reshape(*whole, width).transpose(2, 0, 1, 3, 4)

    band_rows = 2
    grid_cols = patch_dev // band_rows
    band = mixed.reshape(date_dev, band_rows, grid_cols, width)
    axes = ("zl", "y", "c")
    core = lax.axis_index("c")
    first, last = band[:, :1], band[:, -1:]
    near = lax.ppermute(jnp.where(core == 0, last, first), "c", pairs(2, 1))
    across = [(i, i + 1 if i % 2 else i - 1) for i in range(1, 31)]
    far = lax.ppermute(jnp.where(core == 0, first, last), axes, across)
    above, below = jnp.where(core == 0, far, near), jnp.where(core == 0, near, far)
    halo = jnp.concatenate([above, below], axis=1)

    def taps(rows, weights):
        padded = jnp.pad(rows.astype(F32), ((0, 0), (0, 0), (1, 1), (0, 0)))
        return sum(weights[:, i, None] * padded[:, :, i : i + grid_cols] for i in range(3))

    result = band.astype(F32) + conv_bias
    result += taps(band, conv_weight[1:2])
    result += taps(band[:, ::-1], jnp.stack([conv_weight[2], conv_weight[0]]))
    result, halo = tied(result, halo)
    result += taps(halo, jnp.stack([conv_weight[0], conv_weight[2]]))
    return result.astype(BF16).reshape(date_dev, patch_dev, width)


def solution(mesh):
    fine = Mesh(mesh.devices.reshape(2, 4, 4, 4, 2), ("zh", "x", "zl", "y", "c"))
    date, space = ("zh", "x"), ("zl", "y", "c")
    in_specs = (P(date, space, None), P(space, None), P(space, None), P(), P())
    out_specs = P(date, space, None)
    return jax.shard_map(
        shards, mesh=fine, in_specs=in_specs, out_specs=out_specs, check_vma=False
    )
```

```python
import functools
import math

import jax
import jax.numpy as jnp
from jax import lax
from jax.experimental import pallas as pl
from jax.experimental.pallas import tpu as pltpu
from jax.sharding import Mesh
from jax.sharding import PartitionSpec as P

HEADS = 16
GROUP = 8
BF16 = jnp.bfloat16
F32 = jnp.float32


def dot(a, b):
    return jnp.dot(a, b, preferred_element_type=F32)


def attend_rows(queries, keys, values, head_size):
    width = queries.shape[1]
    rows, cols = queries.shape[0], keys.shape[0]
    scale = math.log2(math.e) / math.sqrt(head_size)
    same = (
        lax.broadcasted_iota(jnp.int32, (GROUP, cols), 0)
        == lax.broadcasted_iota(jnp.int32, (GROUP, cols), 1) % GROUP
    )
    others = jnp.where(same, 0.0, -jnp.inf)[None]
    windows, head, heads = [], 0, width // head_size
    while head < heads:
        count = max(1, min((head * head_size // 128 * 128 + 256) // head_size, heads) - head)
        windows.append((min(head * head_size // 128 * 128, width - 256), range(head, head + count)))
        head += count

    def score(base, members):
        lane = lax.broadcasted_iota(jnp.int32, (rows, 256), 1) + base
        query = queries[:, base : base + 256]
        stacked = jnp.concatenate(
            [
                jnp.where(
                    (lane >= h * head_size) & (lane < (h + 1) * head_size),
                    query,
                    jnp.zeros((), BF16),
                )
                for h in members
            ]
        )
        scores = lax.dot_general(
            stacked,
            keys[:, base : base + 256],
            (((1,), (1,)), ((), ())),
            preferred_element_type=F32,
        )
        return (scores.reshape(-1, GROUP, cols) + others).reshape(-1, cols)

    tiles = [None] * (width // 128)

    def gather(base, members, scores):
        top = jnp.max(scores, axis=1, keepdims=True)
        weights = jnp.exp2((scores - top) * scale)
        total = 1.0 / jnp.sum(weights, axis=1, keepdims=True)
        out = dot(weights.astype(BF16), values[:, base : base + 256])
        for i, h in enumerate(members):
            part = slice(i * rows, (i + 1) * rows)
            for tile in range(h * head_size // 128, -(-(h + 1) * head_size // 128)):
                at = tile * 128 - base
                got = out[part, at : at + 128] * total[part]
                if tiles[tile] is None:
                    tiles[tile] = got
                else:
                    lanes = lax.broadcasted_iota(jnp.int32, (rows, 128), 1) + tile * 128
                    tiles[tile] = jnp.where(lanes < h * head_size, tiles[tile], got)

    all_scores = [score(*window) for window in windows]
    yield
    for window, scores in zip(windows, all_scores):
        gather(*window, scores)
    yield jnp.concatenate(tiles, axis=1).astype(BF16)


def weight_copies(w_hbm, core, target, sem):
    half = w_hbm.shape[-1]
    return [
        pltpu.make_async_copy(
            w_hbm.at[mat, row, core],
            target.at[:, row, :, mat * half : (mat + 1) * half],
            sem.at[mat, row],
        )
        for mat in range(3)
        for row in range(4)
    ]


def attend_half(head_size, x_ref, w_ref, out, ready=lambda mat: None):
    width = x_ref.shape[1]
    half = width // 2
    part = out.shape[2]
    turns = 4
    take = 4 // turns

    def project(turn):
        x = x_ref[...].reshape(8, 4, part, width)[:, turn * take : (turn + 1) * take]
        x = x.reshape(8 * take * part, width)
        q = dot(x[: 4 * take * part], w_ref[..., :half].reshape(width, half)).astype(BF16)
        if turn == 0:
            ready(1)
            ready(2)
        kv = dot(x, w_ref[..., half:].reshape(width, width)).astype(BF16)
        shape = (8, take, part, half)
        return q.reshape(4, *shape[1:]), kv[:, :half].reshape(shape), kv[:, half:].reshape(shape)

    def begin(q, k, v):
        steps = attend_rows(*(m.reshape(-1, half) for m in (q, k, v)), head_size)
        next(steps)
        return steps

    ready(0)
    steps = begin(*project(0))
    for turn in range(turns):
        after = begin(*project(turn + 1)) if turn + 1 < turns else None
        out[:, turn] = next(steps).reshape(4, -1, half)
        steps = after


def first_kernel(head_size, x_ref, w_hbm, out, w_next, w_home, w_vm, *sems):
    sem, next_sem, home_sem = sems
    half = w_hbm.shape[-1]
    now = weight_copies(w_hbm, 0, w_vm, sem)
    later = weight_copies(w_hbm, 1, w_next, next_sem)
    for core in range(2):
        for row in range(4):
            later.append(
                pltpu.make_async_copy(
                    w_hbm.at[3, row, core],
                    w_home.at[:, row, :, core * half : (core + 1) * half],
                    home_sem.at[core, row],
                )
            )
    for copy in now:
        copy.start()

    def ready(mat):
        for copy in now[4 * mat : 4 * mat + 4]:
            copy.wait()
        if mat == 2:
            for copy in later:
                copy.start()

    attend_half(head_size, x_ref, w_vm, out, ready)
    for copy in later:
        copy.wait()


def second_kernel(head_size, x_ref, w_ref, out):
    attend_half(head_size, x_ref, w_ref, out)


def run_halves(x, w_all, head_size):
    rows, width = x.shape
    half, part = width // 2, rows // 32
    vmem = pl.BlockSpec(memory_space=pltpu.VMEM)
    attended = jax.ShapeDtypeStruct((4, 4, part, half), BF16)
    columns = (4, 4, width // 16, 3 * half)
    params = pltpu.CompilerParams(vmem_limit_bytes=36 * 1024 * 1024)
    cost = pl.CostEstimate(
        flops=5 * rows * width * half, bytes_accessed=8 * width * half, transcendentals=0
    )
    first, w_next, w_home = pl.pallas_call(
        functools.partial(first_kernel, head_size),
        out_shape=(
            attended,
            pltpu.VMEM(columns, BF16),
            jax.ShapeDtypeStruct((4, 4, width // 16, width), BF16),
        ),
        in_specs=[vmem, pl.BlockSpec(memory_space=pltpu.HBM)],
        out_specs=(vmem, vmem, vmem),
        scratch_shapes=[
            pltpu.VMEM(columns, BF16),
            pltpu.SemaphoreType.DMA((3, 4)),
            pltpu.SemaphoreType.DMA((3, 4)),
            pltpu.SemaphoreType.DMA((2, 4)),
        ],
        compiler_params=params,
        cost_estimate=cost,
    )(x, w_all)
    second = pl.pallas_call(
        functools.partial(second_kernel, head_size),
        out_shape=attended,
        in_specs=[vmem, vmem],
        out_specs=vmem,
        compiler_params=params,
        cost_estimate=pl.CostEstimate(flops=1 << 20, bytes_accessed=1 << 12, transcendentals=0),
    )(x, w_next)
    return [first, second], w_home.reshape(width, width)


def ring(count, shift):
    return [(i, (i + shift) % count) for i in range(count)]


def pairs(count, mask):
    return [(i, i ^ mask) for i in range(count)]


def tied(*values):
    return lax.optimization_barrier(values)


def gather_weights(w_qkv, w_out):
    rows, width = w_out.shape
    half = width // 2
    x, zl, core = lax.axis_index("x"), lax.axis_index("zl"), lax.axis_index("c")
    def columns(at):
        inner = lax.dynamic_slice_in_dim(w_qkv, jnp.minimum(x, 2) * width + at * half, half, 1)
        return jnp.where(x == 3, lax.dynamic_slice_in_dim(w_out, at * half, half, 1), inner)

    keep, give = columns(core), columns(1 - core)
    other = lax.ppermute(give, "c", ring(2, 1))
    piece = jnp.where(
        core == 0, jnp.concatenate([keep, other]), jnp.concatenate([other, keep])
    )
    planes = jnp.zeros((4, 2 * rows, half), BF16)
    planes = lax.dynamic_update_index_in_dim(planes, piece, zl, 0)
    below = [(z, (z + 7) % 8 if z % 2 == 0 else (z + 1) % 8) for z in range(8)]
    for moves, source in (
        (pairs(8, 1), zl ^ 1),
        (below, jnp.where(zl % 2 == 0, zl + 3, zl + 1) % 4),
        (pairs(8, 2), zl ^ 2),
    ):
        got = lax.ppermute(piece, ("zh", "zl"), moves)
        planes = lax.dynamic_update_index_in_dim(planes, got, source, 0)
    gathered = lax.all_gather(planes, ("x", "y", "c"), axis=0, tiled=False)
    return gathered.reshape(4, 4, 2, 4, 2 * rows, half)


def shards(stack, w_qkv, w_out, conv_weight, conv_bias):
    date_dev, patch_dev, width = stack.shape
    head_size = width // HEADS
    x = lax.axis_index("x")
    part = patch_dev // 4

    def cut(mask):
        block = lax.dynamic_slice_in_dim(stack, (x ^ mask) * part, part, axis=1)
        block = block.reshape(date_dev, part // GROUP, GROUP, width).transpose(1, 0, 2, 3)
        return block.reshape(date_dev * part, width)

    masks = (0, 1, 3, 2)
    own = [cut(0)] + [lax.ppermute(cut(m), "x", pairs(4, m)) for m in masks[1:]]
    partner = [lax.ppermute(block, ("zh", "zl"), ring(8, 4)) for block in own]
    w_all = gather_weights(w_qkv, w_out)
    tokens = jnp.concatenate(own + partner)
    halves, w_home = run_halves(tokens, w_all, head_size)

    whole = (4, part // GROUP, date_dev, GROUP)
    total = stack.reshape(date_dev, *whole[:2], GROUP, width).transpose(1, 2, 0, 3, 4)
    total = total.reshape(-1, width).astype(F32)
    for core in range(2):
        attended = halves[core]
        home = jnp.zeros((4, date_dev * part, width // 2), BF16)
        for slot, m in enumerate(masks):
            back = attended[slot].reshape(date_dev * part, width // 2)
            if m:
                back = lax.ppermute(back, "x", pairs(4, m))
            home = lax.dynamic_update_index_in_dim(home, back, x ^ m, 0)
        if core == 0:
            home, halves[1] = tied(home, halves[1])
        columns = slice(core * width // 2, (core + 1) * width // 2)
        total += dot(home.reshape(-1, width // 2), w_home[columns])
    mixed = total.astype(BF16).reshape(*whole, width).transpose(2, 0, 1, 3, 4)

    band_rows = 2
    grid_cols = patch_dev // band_rows
    band = mixed.reshape(date_dev, band_rows, grid_cols, width)
    axes = ("zl", "y", "c")
    core = lax.axis_index("c")
    first, last = band[:, :1], band[:, -1:]
    near = lax.ppermute(jnp.where(core == 0, last, first), "c", pairs(2, 1))
    across = [(i, i + 1 if i % 2 else i - 1) for i in range(1, 31)]
    far = lax.ppermute(jnp.where(core == 0, first, last), axes, across)
    above, below = jnp.where(core == 0, far, near), jnp.where(core == 0, near, far)
    halo = jnp.concatenate([above, below], axis=1)

    def taps(rows, weights):
        padded = jnp.pad(rows.astype(F32), ((0, 0), (0, 0), (1, 1), (0, 0)))
        return sum(weights[:, i, None] * padded[:, :, i : i + grid_cols] for i in range(3))

    result = band.astype(F32) + conv_bias
    result += taps(band, conv_weight[1:2])
    result += taps(band[:, ::-1], jnp.stack([conv_weight[2], conv_weight[0]]))
    result, halo = tied(result, halo)
    result += taps(halo, jnp.stack([conv_weight[0], conv_weight[2]]))
    return result.astype(BF16).reshape(date_dev, patch_dev, width)


def solution(mesh):
    fine = Mesh(mesh.devices.reshape(2, 4, 4, 4, 2), ("zh", "x", "zl", "y", "c"))
    date, space = ("zh", "x"), ("zl", "y", "c")
    in_specs = (P(date, space, None), P(space, None), P(space, None), P(), P())
    out_specs = P(date, space, None)
    return jax.shard_map(
        shards, mesh=fine, in_specs=in_specs, out_specs=out_specs, check_vma=False
    )
```

```python
import functools
import math

import jax
import jax.numpy as jnp
from jax import lax
from jax.experimental import pallas as pl
from jax.experimental.pallas import tpu as pltpu
from jax.sharding import Mesh
from jax.sharding import PartitionSpec as P

HEADS = 16
GROUP = 8
BF16 = jnp.bfloat16
F32 = jnp.float32


def dot(a, b):
    return jnp.dot(a, b, preferred_element_type=F32)


def attend_rows(queries, keys, values, head_size):
    width = queries.shape[1]
    rows, cols = queries.shape[0], keys.shape[0]
    scale = math.log2(math.e) / math.sqrt(head_size)
    same = (
        lax.broadcasted_iota(jnp.int32, (GROUP, cols), 0)
        == lax.broadcasted_iota(jnp.int32, (GROUP, cols), 1) % GROUP
    )
    others = jnp.where(same, 0.0, -jnp.inf)[None]
    windows, head, heads = [], 0, width // head_size
    while head < heads:
        count = max(1, min((head * head_size // 128 * 128 + 256) // head_size, heads) - head)
        windows.append((min(head * head_size // 128 * 128, width - 256), range(head, head + count)))
        head += count

    def score(base, members):
        lane = lax.broadcasted_iota(jnp.int32, (rows, 256), 1) + base
        query = queries[:, base : base + 256]
        stacked = jnp.concatenate(
            [
                jnp.where(
                    (lane >= h * head_size) & (lane < (h + 1) * head_size),
                    query,
                    jnp.zeros((), BF16),
                )
                for h in members
            ]
        )
        scores = lax.dot_general(
            stacked,
            keys[:, base : base + 256],
            (((1,), (1,)), ((), ())),
            preferred_element_type=F32,
        )
        return (scores.reshape(-1, GROUP, cols) + others).reshape(-1, cols)

    tiles = [None] * (width // 128)

    def gather(base, members, scores):
        top = jnp.max(scores, axis=1, keepdims=True)
        weights = jnp.exp2((scores - top) * scale)
        total = 1.0 / jnp.sum(weights, axis=1, keepdims=True)
        out = dot(weights.astype(BF16), values[:, base : base + 256])
        for i, h in enumerate(members):
            part = slice(i * rows, (i + 1) * rows)
            for tile in range(h * head_size // 128, -(-(h + 1) * head_size // 128)):
                at = tile * 128 - base
                got = out[part, at : at + 128] * total[part]
                if tiles[tile] is None:
                    tiles[tile] = got
                else:
                    lanes = lax.broadcasted_iota(jnp.int32, (rows, 128), 1) + tile * 128
                    tiles[tile] = jnp.where(lanes < h * head_size, tiles[tile], got)

    all_scores = [score(*window) for window in windows]
    yield
    for window, scores in zip(windows, all_scores):
        gather(*window, scores)
    yield jnp.concatenate(tiles, axis=1).astype(BF16)


def weight_copies(w_hbm, core, target, sem):
    half = w_hbm.shape[-1]
    return [
        pltpu.make_async_copy(
            w_hbm.at[mat, row, core],
            target.at[:, row, :, mat * half : (mat + 1) * half],
            sem.at[mat, row],
        )
        for mat in range(3)
        for row in range(4)
    ]


def attend_half(head_size, x_ref, w_ref, out, ready=lambda mat: None):
    width = x_ref.shape[1]
    half = width // 2
    part = out.shape[2]
    turns = 4
    take = 4 // turns

    def project(turn):
        x = x_ref[...].reshape(8, 4, part, width)[:, turn * take : (turn + 1) * take]
        x = x.reshape(8 * take * part, width)
        q = dot(x[: 4 * take * part], w_ref[..., :half].reshape(width, half)).astype(BF16)
        if turn == 0:
            ready(1)
            ready(2)
        kv = dot(x, w_ref[..., half:].reshape(width, width)).astype(BF16)
        shape = (8, take, part, half)
        return q.reshape(4, *shape[1:]), kv[:, :half].reshape(shape), kv[:, half:].reshape(shape)

    def begin(q, k, v):
        steps = attend_rows(*(m.reshape(-1, half) for m in (q, k, v)), head_size)
        next(steps)
        return steps

    ready(0)
    steps = begin(*project(0))
    for turn in range(turns):
        after = begin(*project(turn + 1)) if turn + 1 < turns else None
        out[:, turn] = next(steps).reshape(4, -1, half)
        steps = after


def first_kernel(head_size, x_ref, w_hbm, out, w_next, w_home, w_vm, *sems):
    sem, next_sem, home_sem = sems
    half = w_hbm.shape[-1]
    now = weight_copies(w_hbm, 0, w_vm, sem)
    later = weight_copies(w_hbm, 1, w_next, next_sem)
    for core in range(2):
        for row in range(4):
            later.append(
                pltpu.make_async_copy(
                    w_hbm.at[3, row, core],
                    w_home.at[:, row, :, core * half : (core + 1) * half],
                    home_sem.at[core, row],
                )
            )
    for copy in now:
        copy.start()

    def ready(mat):
        for copy in now[4 * mat : 4 * mat + 4]:
            copy.wait()
        if mat == 2:
            for copy in later:
                copy.start()

    attend_half(head_size, x_ref, w_vm, out, ready)
    for copy in later:
        copy.wait()


def second_kernel(head_size, x_ref, w_ref, out):
    attend_half(head_size, x_ref, w_ref, out)


def run_halves(x, w_all, head_size):
    rows, width = x.shape
    half, part = width // 2, rows // 32
    vmem = pl.BlockSpec(memory_space=pltpu.VMEM)
    attended = jax.ShapeDtypeStruct((4, 4, part, half), BF16)
    columns = (4, 4, width // 16, 3 * half)
    params = pltpu.CompilerParams(vmem_limit_bytes=36 * 1024 * 1024)
    cost = pl.CostEstimate(
        flops=5 * rows * width * half, bytes_accessed=8 * width * half, transcendentals=0
    )
    first, w_next, w_home = pl.pallas_call(
        functools.partial(first_kernel, head_size),
        out_shape=(
            attended,
            pltpu.VMEM(columns, BF16),
            jax.ShapeDtypeStruct((4, 4, width // 16, width), BF16),
        ),
        in_specs=[vmem, pl.BlockSpec(memory_space=pltpu.HBM)],
        out_specs=(vmem, vmem, vmem),
        scratch_shapes=[
            pltpu.VMEM(columns, BF16),
            pltpu.SemaphoreType.DMA((3, 4)),
            pltpu.SemaphoreType.DMA((3, 4)),
            pltpu.SemaphoreType.DMA((2, 4)),
        ],
        compiler_params=params,
        cost_estimate=cost,
    )(x, w_all)
    second = pl.pallas_call(
        functools.partial(second_kernel, head_size),
        out_shape=attended,
        in_specs=[vmem, vmem],
        out_specs=vmem,
        compiler_params=params,
        cost_estimate=pl.CostEstimate(flops=1 << 20, bytes_accessed=1 << 12, transcendentals=0),
    )(x, w_next)
    return [first, second], w_home.reshape(width, width)


def ring(count, shift):
    return [(i, (i + shift) % count) for i in range(count)]


def pairs(count, mask):
    return [(i, i ^ mask) for i in range(count)]


def tied(*values):
    return lax.optimization_barrier(values)


def gather_weights(w_qkv, w_out):
    rows, width = w_out.shape
    half = width // 2
    x, zl, core = lax.axis_index("x"), lax.axis_index("zl"), lax.axis_index("c")
    def columns(at):
        inner = lax.dynamic_slice_in_dim(w_qkv, jnp.minimum(x, 2) * width + at * half, half, 1)
        return jnp.where(x == 3, lax.dynamic_slice_in_dim(w_out, at * half, half, 1), inner)

    keep, give = columns(core), columns(1 - core)
    other = lax.ppermute(give, "c", ring(2, 1))
    piece = jnp.where(
        core == 0, jnp.concatenate([keep, other]), jnp.concatenate([other, keep])
    )
    planes = jnp.zeros((4, 2 * rows, half), BF16)
    planes = lax.dynamic_update_index_in_dim(planes, piece, zl, 0)
    below = [(z, (z + 7) % 8 if z % 2 == 0 else (z + 1) % 8) for z in range(8)]
    for moves, source in (
        (pairs(8, 1), zl ^ 1),
        (below, jnp.where(zl % 2 == 0, zl + 3, zl + 1) % 4),
        (pairs(8, 2), zl ^ 2),
    ):
        got = lax.ppermute(piece, ("zh", "zl"), moves)
        planes = lax.dynamic_update_index_in_dim(planes, got, source, 0)
    gathered = lax.all_gather(planes, ("x", "y", "c"), axis=0, tiled=False)
    return gathered.reshape(4, 4, 2, 4, 2 * rows, half)


def shards(stack, w_qkv, w_out, conv_weight, conv_bias):
    date_dev, patch_dev, width = stack.shape
    head_size = width // HEADS
    x = lax.axis_index("x")
    part = patch_dev // 4

    def cut(mask):
        block = lax.dynamic_slice_in_dim(stack, (x ^ mask) * part, part, axis=1)
        block = block.reshape(date_dev, part // GROUP, GROUP, width).transpose(1, 0, 2, 3)
        return block.reshape(date_dev * part, width)

    masks = (0, 2, 1, 3)
    own = [cut(0)] + [lax.ppermute(cut(m), "x", pairs(4, m)) for m in masks[1:]]
    partner = [lax.ppermute(block, ("zh", "zl"), ring(8, 4)) for block in own]
    w_all = gather_weights(w_qkv, w_out)
    tokens = jnp.concatenate(own + partner)
    halves, w_home = run_halves(tokens, w_all, head_size)

    whole = (4, part // GROUP, date_dev, GROUP)
    total = stack.reshape(date_dev, *whole[:2], GROUP, width).transpose(1, 2, 0, 3, 4)
    total = total.reshape(-1, width).astype(F32)
    for core in range(2):
        attended = halves[core]
        home = jnp.zeros((4, date_dev * part, width // 2), BF16)
        for slot, m in enumerate(masks):
            back = attended[slot].reshape(date_dev * part, width // 2)
            if m:
                back = lax.ppermute(back, "x", pairs(4, m))
            home = lax.dynamic_update_index_in_dim(home, back, x ^ m, 0)
        if core == 0:
            home, halves[1] = tied(home, halves[1])
        columns = slice(core * width // 2, (core + 1) * width // 2)
        total += dot(home.reshape(-1, width // 2), w_home[columns])
    mixed = total.astype(BF16).reshape(*whole, width).transpose(2, 0, 1, 3, 4)

    band_rows = 2
    grid_cols = patch_dev // band_rows
    band = mixed.reshape(date_dev, band_rows, grid_cols, width)
    axes = ("zl", "y", "c")
    core = lax.axis_index("c")
    first, last = band[:, :1], band[:, -1:]
    near = lax.ppermute(jnp.where(core == 0, last, first), "c", pairs(2, 1))
    across = [(i, i + 1 if i % 2 else i - 1) for i in range(1, 31)]
    far = lax.ppermute(jnp.where(core == 0, first, last), axes, across)
    above, below = jnp.where(core == 0, far, near), jnp.where(core == 0, near, far)
    halo = jnp.concatenate([above, below], axis=1)

    def taps(rows, weights):
        padded = jnp.pad(rows.astype(F32), ((0, 0), (0, 0), (1, 1), (0, 0)))
        return sum(weights[:, i, None] * padded[:, :, i : i + grid_cols] for i in range(3))

    result = band.astype(F32) + conv_bias
    result += taps(band, conv_weight[1:2])
    result += taps(band[:, ::-1], jnp.stack([conv_weight[2], conv_weight[0]]))
    result, halo = tied(result, halo)
    result += taps(halo, jnp.stack([conv_weight[0], conv_weight[2]]))
    return result.astype(BF16).reshape(date_dev, patch_dev, width)


def solution(mesh):
    fine = Mesh(mesh.devices.reshape(2, 4, 4, 4, 2), ("zh", "x", "zl", "y", "c"))
    date, space = ("zh", "x"), ("zl", "y", "c")
    in_specs = (P(date, space, None), P(space, None), P(space, None), P(), P())
    out_specs = P(date, space, None)
    return jax.shard_map(
        shards, mesh=fine, in_specs=in_specs, out_specs=out_specs, check_vma=False
    )
```
